32 devices in a mesh: section: 2 (over core), tok: 4 (over z), head: 4 (over y, x).
Axes of the slice: x: 2, y: 2, z: 4, core: 2. Of those that a mesh axis runs over, the one named last changes fastest.
Arguments:
- block_input: bfloat16 [2, 1024, 2048], P(None, 'tok'), may hold values from -6 to 6
- out_grad: bfloat16 [2, 1024, 2048], P(None, 'tok'), may hold values from -6 to 6
- lengths: int32 [2, 4], replicated, may hold values from 1 to 1021, as said below
- norm_gain: float32 [2, 2048], P('section'), may hold values from 0.5 to 1.5
- gate_weight: bfloat16 [2, 2048, 4096], P('section', None, 'head'), may hold values from -0.125 to 0.125
- value_weight: bfloat16 [2, 2048, 4096], P('section', None, 'head'), may hold values from -0.125 to 0.125
- select_weight: bfloat16 [2, 2048, 256], P('section'), may hold values from -0.125 to 0.125
- step_weight: bfloat16 [2, 2048, 64], P('section', None, 'head'), may hold values from -0.25 to 0.25
- conv_value: float32 [2, 4, 64, 64], P('section', None, 'head'), may hold values from -3 to 3
- conv_value_bias: float32 [2, 64, 64], P('section', 'head'), may hold values from -2 to 2
- conv_select: float32 [2, 4, 256], P('section'), may hold values from -3 to 3
- conv_select_bias: float32 [2, 256], P('section'), may hold values from -2 to 2
- step_bias: float32 [2, 64], P('section', 'head'), may hold values from -6 to -2
- log_rate: float32 [2, 64], P('section', 'head'), may hold values from -8 to 1.5
- skip_gain: float32 [2, 64], P('section', 'head'), may hold values from 0.5 to 1.5
- gate_gain: float32 [2, 64, 64], P('section', 'head'), may hold values from 0.5 to 1.5
- output_weight: bfloat16 [2, 4096, 2048], P('section', 'head'), may hold values from -0.09375 to 0.09375
Outputs:
- layer_out: float32 [2, 2, 1024, 2048], P('section', None, 'tok')
- input_grad: float32 [2, 2, 1024, 2048], P('section', None, 'tok')
- norm_gain_grad: float32 [2, 2048], P('section', 'tok')
- gate_weight_grad: float32 [2, 2048, 4096], P('section', 'tok', 'head')
- value_weight_grad: float32 [2, 2048, 4096], P('section', 'tok', 'head')
- select_weight_grad: float32 [2, 2048, 256], P('section', 'tok')
- step_weight_grad: float32 [2, 2048, 64], P('section', 'tok', 'head')
- conv_value_grad: float32 [2, 4, 64, 64], P('section', None, 'head', 'tok')
- conv_value_bias_grad: float32 [2, 64, 64], P('section', 'head', 'tok')
- conv_select_grad: float32 [2, 4, 256], P('section', None, 'tok')
- conv_select_bias_grad: float32 [2, 256], P('section', 'tok')
- step_bias_grad: float32 [2, 64], P('section', 'head')
- log_rate_grad: float32 [2, 64], P('section', 'head')
- skip_gain_grad: float32 [2, 64], P('section', 'head')
- gate_gain_grad: float32 [2, 64, 64], P('section', 'head', 'tok')
- output_weight_grad: float32 [2, 4096, 2048], P('section', 'head', 'tok')
The draws below stay inside these ranges and needn't reach their ends.
Inputs may be any that keep to these rules, and one draw needn't show every extreme that they name: Each row lists the lengths of 4 sequences packed in order into the 1024 rows of a micro-batch and sums to 1024; one of them, at a place drawn anew, holds all but fewer than 256 rows, so it starts in the first 256 rows and ends in the last 256 rows; in one micro-batch all others have length 1.
All inputs are finite; a program needn't handle non-finite values.
Results may differ from the reference program's by a relative error of at most 0.012.
The reference program's roundings to bfloat16 on the way count: a program that leaves them out, or rounds other values in their place, can miss the bound.
Values sent between devices are 32-bit elements; how exact they have to be, the bound alone decides.
No kernel may reach another device: no remote copies, remote signals or barrier semaphores. Data moves between devices by JAX's collectives and lax.ppermute only.
A program may use at most 192 MiB of HBM per device.

```python
import jax
import jax.numpy as jnp
from jax import lax

D = 2048
H = 64
P_SIZE = 64
NST = 128
K = 4
BLOCK = 256
MB_TOK = 256
MICRO = 2
SEQS = 4
DI = 4096
TOKENS = 1024
N_SECTION = 2


def draw_lengths(key, part):
    key = jax.random.fold_in(key, 11)
    short_key, place_key, row_key = jax.random.split(key, 3)
    shorts = jax.random.randint(short_key, (MICRO, SEQS), 1, MB_TOK // SEQS + 1)
    full_row = jax.random.randint(row_key, (), 0, MICRO)
    shorts = jnp.where(jnp.arange(MICRO)[:, None] == full_row, 1, shorts)
    long_place = jax.random.randint(place_key, (MICRO, 1), 0, SEQS)
    is_long = jnp.arange(SEQS)[None, :] == long_place
    short_total = jnp.sum(jnp.where(is_long, 0, shorts), axis=1, keepdims=True)
    return jnp.where(is_long, TOKENS - short_total, shorts).astype(jnp.int32)


def level_of(rng, shape, shards, least, top_value):
    loudness = 1.0
    for position, shards_of in shards:
        steps = jax.random.uniform(jax.random.fold_in(jax.random.fold_in(rng, 6), position), (shards_of,), jnp.float32, least / len(shards), top_value / len(shards))
        loudness = loudness * jnp.repeat(jnp.exp(steps), shape[position] // shards_of).reshape((-1,) + (1,) * (len(shape) - 1 - position))
    return loudness


def gaussian(key, shape, deviation, reach, cuts=(), kind=jnp.bfloat16):
    drawn = jax.random.normal(key, shape, jnp.float32) * deviation
    if len(cuts) > 0:
        drawn = level_of(key, shape, cuts, -0.22, 0.18) * drawn
    return jnp.clip(drawn, min=-reach, max=reach).astype(kind)


def setup_inputs(seed: int = 0) -> dict:
    splits = jax.random.split(jax.random.key(seed), 18)
    return {
        "block_input": gaussian(splits[0], (MICRO, TOKENS, D), 1.0, 6.0, ((1, 4),)),
        "out_grad": gaussian(splits[1], (MICRO, TOKENS, D), 1.0, 6.0, ((1, 4),)),
        "lengths": draw_lengths(jax.random.fold_in(splits[17], 71), 0),
        "norm_gain": jnp.clip(1.0 + 0.1 * jax.random.normal(splits[3], (N_SECTION, D), jnp.float32), 0.5, 1.5),
        "gate_weight": gaussian(splits[4], (N_SECTION, D, DI), D ** -0.5, 0.125, ((0, 2), (2, 4))),
        "value_weight": gaussian(splits[5], (N_SECTION, D, DI), D ** -0.5, 0.125, ((0, 2), (2, 4))),
        "select_weight": gaussian(splits[6], (N_SECTION, D, 2 * NST), D ** -0.5, 0.125, ((0, 2),)),
        "step_weight": gaussian(splits[7], (N_SECTION, D, H), (D // 4) ** -0.5, 0.25, ((0, 2), (2, 4))),
        "conv_value": gaussian(splits[8], (N_SECTION, K, H, P_SIZE), 0.5, 3.0, ((0, 2), (2, 4)), jnp.float32),
        "conv_value_bias": gaussian(splits[9], (N_SECTION, H, P_SIZE), 0.3, 2.0, ((0, 2), (1, 4)), jnp.float32),
        "conv_select": gaussian(splits[10], (N_SECTION, K, 2 * NST), 0.5, 3.0, ((0, 2),), jnp.float32),
        "conv_select_bias": gaussian(splits[11], (N_SECTION, 2 * NST), 0.3, 2.0, ((0, 2),), jnp.float32),
        "step_bias": jnp.clip(-6.0 + 4.0 * jax.random.uniform(splits[12], (N_SECTION, H), jnp.float32) ** level_of(splits[12], (N_SECTION, H), ((0, 2), (1, 4)), -0.2, 0.2), -6.0, -2.0),
        "log_rate": jnp.clip(-8.0 + 9.5 * jax.random.uniform(splits[13], (N_SECTION, H), jnp.float32) ** level_of(splits[13], (N_SECTION, H), ((0, 2), (1, 4)), -0.2, 0.2), -8.0, 1.5),
        "skip_gain": jnp.clip(0.5 + 1.0 * jax.random.uniform(splits[14], (N_SECTION, H), jnp.float32) ** level_of(splits[14], (N_SECTION, H), ((0, 2), (1, 4)), -0.2, 0.2), 0.5, 1.5),
        "gate_gain": jnp.clip(1.0 + 0.1 * jax.random.normal(splits[15], (N_SECTION, H, P_SIZE), jnp.float32), 0.5, 1.5),
        "output_weight": gaussian(splits[16], (N_SECTION, DI, D), DI ** -0.5, 0.09375, ((0, 2), (1, 4))),
    }


EPSILON = 1e-05
PRECISE = lax.Precision.HIGHEST

@jax.custom_vjp
def low(v):
    return lax.optimization_barrier(v.astype(jnp.bfloat16)).astype(jnp.float32)

@jax.custom_vjp
def low_back(v):
    return v

def low_keep(v):
    return (low(v), None)

def low_pass(kept, grad):
    return (grad,)

def back_keep(v):
    return (v, None)

def back_low(kept, grad):
    return (low(grad),)
low.defvjp(low_keep, low_pass)
low_back.defvjp(back_keep, back_low)

def seg_of(points, seq_ends):
    inside = lax.optimization_barrier(jnp.sum((points[:, None] >= seq_ends[None, :]).astype(jnp.int32), axis=1)).astype(jnp.int32)
    return jnp.where(points >= 0, inside, -1).astype(jnp.int32)

def ssd_blocks(x_act, b_act, c_act, step_size, log_decay, segment, seg_prev, start_state):
    block_count = x_act.shape[0] // BLOCK
    heads_here = log_decay.shape[1]
    block_items = (x_act.reshape(block_count, BLOCK, heads_here, P_SIZE), b_act.reshape(block_count, BLOCK, NST), c_act.reshape(block_count, BLOCK, NST), step_size.reshape(block_count, BLOCK, heads_here), log_decay.reshape(block_count, BLOCK, heads_here), segment.reshape(block_count, BLOCK), seg_prev.reshape(block_count, BLOCK)[:, 0])

    def one_block(carried, items):
        x_rows, b_rows, c_rows, step_rows, decay_rows, seg_rows, seg_before = items
        cum_decay = jnp.cumsum(decay_rows, axis=0)
        row_ids = jnp.arange(BLOCK)
        mask_rows = ((seg_rows[:, None] == seg_rows[None, :]) & (row_ids[:, None] >= row_ids[None, :])).astype(jnp.float32)
        cum_heads = cum_decay.T
        decay_matrix = jnp.exp(jnp.where(mask_rows[None] > 0, cum_heads[:, :, None] - cum_heads[:, None, :], 0.0)) * mask_rows[None]
        scores = jnp.dot(c_rows, b_rows.T, precision=PRECISE)
        mixing = decay_matrix * scores[None] * step_rows.T[:, None, :]
        block_out = jnp.einsum('hts,shp->thp', mixing, x_rows, precision=PRECISE)
        carry_in = (seg_rows == seg_before).astype(jnp.float32)
        decay_in = jnp.exp(cum_decay) * carry_in[:, None]
        block_out = block_out + jnp.einsum('tn,hpn->thp', c_rows, carried, precision=PRECISE) * decay_in[:, :, None]
        tail_mask = (seg_rows == seg_rows[-1]).astype(jnp.float32)
        end_weight = jnp.exp(cum_decay[-1][None, :] - cum_decay) * tail_mask[:, None] * step_rows
        fresh_state = carried * decay_in[-1][:, None, None] + jnp.einsum('sh,sn,shp->hpn', end_weight, b_rows, x_rows, precision=PRECISE)
        return (fresh_state, block_out)
    last_state, outputs = lax.scan(jax.checkpoint(one_block), start_state, block_items)
    return (outputs.reshape(x_act.shape[0], heads_here * P_SIZE), last_state)

def layer_forward(hidden_in, weights, segment, seg_prev, tap_masks):
    norm_gain, gate_weight, value_weight, select_weight, step_weight, conv_value, conv_value_bias, conv_select, conv_select_bias, step_bias, log_rate, skip_gain, gate_gain, output_weight = weights
    row_count = hidden_in.shape[0]
    value_width = H * P_SIZE
    normed = low(hidden_in * lax.rsqrt(lax.optimization_barrier(jnp.mean(hidden_in * hidden_in, axis=-1, keepdims=True)) + EPSILON) * norm_gain)
    gate_pre = low_back(jnp.dot(normed, gate_weight, precision=PRECISE))
    value_pre = low_back(jnp.dot(normed, value_weight, precision=PRECISE))
    select_pre = low_back(jnp.dot(normed, select_weight, precision=PRECISE))
    step_pre = low_back(jnp.dot(normed, step_weight, precision=PRECISE))
    conv_input = jnp.concatenate([value_pre, select_pre], axis=1)
    kernel = jnp.concatenate([conv_value.reshape(K, value_width), conv_select], axis=1)
    kernel_bias = jnp.concatenate([conv_value_bias.reshape(value_width), conv_select_bias])
    padded = jnp.pad(conv_input, ((K - 1, 0), (0, 0)))
    conv_total = jnp.broadcast_to(kernel_bias[None, :], conv_input.shape)
    for tap_index in range(K):
        conv_total = conv_total + kernel[tap_index][None, :] * padded[tap_index:tap_index + row_count] * tap_masks[tap_index][:, None]
    activated = jax.nn.silu(conv_total)
    x_act = activated[:, :value_width]
    b_act = activated[:, value_width:value_width + NST]
    c_act = activated[:, value_width + NST:]
    step_size = jax.nn.softplus(step_pre + step_bias)
    log_decay = -jnp.exp(log_rate) * step_size
    scan_out, last_state = ssd_blocks(x_act, b_act, c_act, step_size, log_decay, segment, seg_prev, jnp.zeros((H, P_SIZE, NST), jnp.float32))
    scan_out = scan_out + (x_act.reshape(row_count, H, P_SIZE) * skip_gain[None, :, None]).reshape(row_count, value_width)
    gated_value = scan_out * jax.nn.silu(gate_pre)
    scaled = low(gated_value * lax.rsqrt(lax.optimization_barrier(jnp.mean(gated_value * gated_value, axis=-1, keepdims=True)) + EPSILON) * gate_gain.reshape(value_width))
    branch = low_back(jnp.dot(scaled, output_weight, precision=PRECISE))
    return hidden_in + branch

def reference(block_input, out_grad, lengths, norm_gain, gate_weight, value_weight, select_weight, step_weight, conv_value, conv_value_bias, conv_select, conv_select_bias, step_bias, log_rate, skip_gain, gate_gain, output_weight):
    params = tuple((weight.astype(jnp.float32) for weight in (norm_gain, gate_weight, value_weight, select_weight, step_weight, conv_value, conv_value_bias, conv_select, conv_select_bias, step_bias, log_rate, skip_gain, gate_gain, output_weight)))
    inputs = block_input.astype(jnp.float32)
    positions = jnp.arange(TOKENS).astype(jnp.int32)
    contexts = []
    for micro_index in range(MICRO):
        seq_ends = jnp.cumsum(lengths[micro_index]).astype(jnp.int32)
        segment = seg_of(positions, seq_ends)
        seg_prev = seg_of(positions - 1, seq_ends)
        tap_masks = jnp.stack([(seg_of(positions - (K - 1 - tap_index), seq_ends) == segment).astype(jnp.float32) for tap_index in range(K)])
        contexts.append((segment, seg_prev, tap_masks))

    def run_layers(weights_all, first_inputs, between):
        firsts = []
        seconds = []
        first_layer = tuple((weight[0] for weight in weights_all))
        second_layer = tuple((weight[1] for weight in weights_all))
        for micro_index in range(MICRO):
            segment, seg_prev, tap_masks = contexts[micro_index]
            middle = layer_forward(first_inputs[micro_index], first_layer, segment, seg_prev, tap_masks) + between[micro_index]
            firsts.append(middle)
            seconds.append(layer_forward(middle, second_layer, segment, seg_prev, tap_masks))
        return (jnp.stack(firsts), jnp.stack(seconds))
    between = jnp.zeros_like(inputs)
    (firsts, seconds), pullback = jax.vjp(run_layers, params, inputs, between)
    param_grads, input_part, between_part = pullback((jnp.zeros_like(firsts), out_grad.astype(jnp.float32)))
    layer_out = jnp.stack([firsts, seconds])
    input_grad = jnp.stack([input_part, between_part])
    return (layer_out, input_grad, param_grads[0], param_grads[1], param_grads[2], param_grads[3], param_grads[4], param_grads[5], param_grads[6], param_grads[7], param_grads[8], param_grads[9], param_grads[10], param_grads[11], param_grads[12], param_grads[13])
```

```python
from functools import partial
from types import SimpleNamespace

import jax
import jax.numpy as jnp
from jax import lax
from jax.experimental import pallas as pl
from jax.experimental.pallas import tpu as pltpu
from jax.sharding import PartitionSpec as P

D = 2048
H = 64
P_SIZE = 64
NST = 128
K = 4
EPSILON = 1e-05
SECTION, TOK, HEAD = AXES = ("section", "tok", "head")
F32 = jnp.float32
BF16 = jnp.bfloat16
EXACT = lax.Precision.HIGHEST
VMEM_BYTES = 58 * 1024 * 1024
PAD = 128

DT, CUM, SIG, LOG, ENDW, DECIN, BASE = (0, 16, 32, 48, 64, 80, 96)


def send(value, section, move):
    tok_count, head_count = (lax.axis_size(TOK), lax.axis_size(HEAD))

    def flat(tok, head):
        return (section * tok_count + tok) * head_count + head

    pairs = []
    for tok in range(tok_count):
        for head in range(head_count):
            target = move(tok, head)
            if 0 <= target[0] < tok_count:
                pairs.append((flat(tok, head), flat(*target)))
    return lax.ppermute(value, AXES, pairs)


def to_head(value, section, step):
    return send(value, section, lambda tok, head: (tok, head ^ step))


def to_tok(value, section, step):
    return send(value, section, lambda tok, head: (tok + step, head))


def nn(left, right, precision=None):
    return lax.dot_general(
        left, right, (((1,), (0,)), ((), ())), precision=precision, preferred_element_type=F32
    )


def nt(left, right, precision=None):
    return lax.dot_general(
        left, right, (((1,), (1,)), ((), ())), precision=precision, preferred_element_type=F32
    )


def tn(left, right):
    return lax.dot_general(left, right, (((0,), (0,)), ((), ())), preferred_element_type=F32)


def split(values):
    high = values.astype(BF16)
    return (high, (values - high.astype(F32)).astype(BF16))


def fine(product, left, right):
    return product(left[0], right[0]) + (product(left[0], right[1]) + product(left[1], right[0]))


def act_of(values):
    return values * sigmoid(values)


def sigmoid(values):
    return 1.0 / (1.0 + jnp.exp(-values))


def seg_at(points, ends, micro):
    inside = (points >= ends[micro, 0]).astype(jnp.int32)
    for which in range(1, 4):
        inside = inside + (points >= ends[micro, which]).astype(jnp.int32)
    return jnp.where(points >= 0, inside, -1)


def call(body, grid, scalars, ins, in_specs, outs, out_specs, scratch=(), flops=0, name=None):
    flag = len(scalars) - 1

    def guarded(*refs):
        @pl.when(refs[flag][4] == 1)
        def _():
            body(*refs)

    moved = sum(a.size * a.dtype.itemsize for a in ins)
    moved += sum(o.size * o.dtype.itemsize for o in outs)
    return pl.pallas_call(
        guarded,
        grid_spec=pltpu.PrefetchScalarGridSpec(
            num_scalar_prefetch=len(scalars),
            grid=grid,
            in_specs=in_specs,
            out_specs=out_specs,
            scratch_shapes=list(scratch),
        ),
        out_shape=outs,
        compiler_params=pltpu.CompilerParams(vmem_limit_bytes=VMEM_BYTES),
        cost_estimate=pl.CostEstimate(flops=flops, bytes_accessed=moved, transcendentals=0),
        name=name,
    )(*scalars, *ins)


def rows(count, width):
    return pl.BlockSpec((count, width), lambda m, *_: (m, 0))


def whole(shape):
    return pl.BlockSpec(shape, lambda m, *_: (0,) * len(shape))


def struct(shape, dtype=F32):
    return jax.ShapeDtypeStruct(shape, dtype)


def pair_of(table, base, pair, lane):
    first = table[:, base + 2 * pair : base + 2 * pair + 1]
    second = table[:, base + 2 * pair + 1 : base + 2 * pair + 2]
    return jnp.where(lane < P_SIZE, first, second)


def head_sums(values, pair, head_count):
    owner = lax.broadcasted_iota(jnp.int32, (head_count, 2 * P_SIZE), 0)
    lane = lax.broadcasted_iota(jnp.int32, (head_count, 2 * P_SIZE), 1)
    chosen = (owner == 2 * pair + (lane >= P_SIZE).astype(jnp.int32)).astype(BF16)
    high = values.astype(BF16)
    low = (values - high.astype(F32)).astype(BF16)
    return nt(chosen, high) + nt(chosen, low)


def in_body(idx, *refs, part_count, micro_count, row_count):
    parts, refs = (refs[:part_count], refs[part_count:])
    gain, w_value, w_select, w_step, normed, value, select, step = refs
    chunk = row_count // 4
    step_id = pl.program_id(0)

    @pl.when(step_id == 0)
    def _():
        for micro in range(micro_count):
            for piece in range(4):
                if part_count == 1:
                    place = micro * row_count + piece * chunk
                    values = parts[0][place : place + chunk, :].astype(F32)
                else:
                    place = pl.multiple_of(micro * row_count + (idx[1] ^ piece) * chunk, chunk)
                    values = parts[piece][micro * chunk : (micro + 1) * chunk, :]
                inv = lax.rsqrt(jnp.mean(values * values, axis=-1, keepdims=True) + EPSILON)
                normed[pl.ds(place, chunk), :] = (values * inv * gain[...]).astype(BF16)
        select[...] = nn(normed[...], w_select[...])
        step[...] = nn(normed[...], w_step[...])

    value[...] = nn(normed[...], w_value[...])


def in_project(idx, parts, weights, micro_count, row_count):
    total = micro_count * row_count
    width = weights.value.shape[1]
    heads = weights.step.shape[1]
    tile = width // 4
    outs = [
        struct((total, D), BF16),
        struct((total, width)),
        struct((total, 2 * NST)),
        struct((total, heads)),
    ]
    cols = pl.BlockSpec((total, tile), lambda j, *_: (0, j))
    wcols = pl.BlockSpec((D, tile), lambda j, *_: (0, j))
    return call(
        partial(in_body, part_count=len(parts), micro_count=micro_count, row_count=row_count),
        (4,),
        (idx,),
        [*parts, weights.gain, weights.value, weights.select, weights.step],
        [whole(part.shape) for part in parts]
        + [whole((1, D)), wcols, whole((D, 2 * NST)), whole((D, heads))],
        outs,
        [whole((total, D)), cols, whole((total, 2 * NST)), whole((total, heads))],
        flops=2 * total * D * (width + 2 * NST),
    )


def gate_body(idx, normed, w_gate, gate):
    gate[...] = nn(normed[...], w_gate[...])


def gate_project(idx, normed, w_gate):
    total, width = (normed.shape[0], w_gate.shape[1])
    tile = width // 4
    return call(
        gate_body,
        (4,),
        (idx,),
        [normed, w_gate],
        [whole((total, D)), pl.BlockSpec((D, tile), lambda j, *_: (0, j))],
        [struct((total, width))],
        [pl.BlockSpec((total, tile), lambda j, *_: (0, j))],
        flops=2 * total * D * width,
    )[0]


def conv_body(
    ends, idx, value, select, step, halo, taps, head_rows,
    conv, table, table_t, state, extended, weighted, weighted_low,
):
    micro = pl.program_id(0)
    row_count, width = value.shape
    heads = step.shape[1]
    base = idx[0]
    at = base + lax.broadcasted_iota(jnp.int32, (row_count, 1), 0)
    seg = seg_at(at, ends, micro)
    seg_before = seg_at(base - 1 + jnp.zeros((1, 1), jnp.int32), ends, micro)
    seg_last = seg_at(base + row_count - 1 + jnp.zeros((1, 1), jnp.int32), ends, micro)
    carry = (seg == seg_before).astype(F32)
    tail = (seg == seg_last).astype(F32)

    pre = step[...] + head_rows[0:1, 0:heads]
    step_size = jnp.maximum(pre, 0.0) + jnp.log1p(jnp.exp(-jnp.abs(pre)))
    log_decay = -jnp.exp(head_rows[1:2, 0:heads]) * step_size
    row_id = lax.broadcasted_iota(jnp.int32, (row_count, row_count), 0)
    col_id = lax.broadcasted_iota(jnp.int32, (row_count, row_count), 1)
    cum = nn((row_id >= col_id).astype(F32), log_decay, EXACT)
    end_base = jnp.exp(cum[row_count - 1 : row_count, :] - cum) * tail
    decay_in = jnp.exp(cum) * carry
    table[...] = jnp.zeros_like(table)
    for place, part in (
        (DT, step_size),
        (CUM, cum),
        (SIG, sigmoid(pre)),
        (LOG, log_decay),
        (ENDW, end_base * step_size),
        (DECIN, decay_in),
        (BASE, end_base),
    ):
        table[:, place : place + heads] = part
    table_t[...] = table[...].T

    extended[0:8, :] = halo[...]
    extended[8:, 0:width] = value[...]
    extended[8:, width:] = select[...]
    masks = [(seg_at(at - (K - 1 - tap), ends, micro) == seg).astype(F32) for tap in range(K - 1)]
    lane = lax.broadcasted_iota(jnp.int32, (row_count, 128), 1)
    columns = width + 2 * NST
    for left in range(0, columns, 128):
        span = slice(left, left + 128)
        total = taps[4:5, span] + taps[3:4, span] * extended[8 : 8 + row_count, span]
        for tap in range(K - 1):
            total = total + taps[tap : tap + 1, span] * (
                extended[5 + tap : 5 + tap + row_count, span] * masks[tap]
            )
        conv[:, span] = total
        if left < width:
            weighted[:, span], weighted_low[:, span] = split(
                act_of(total) * pair_of(table[...], ENDW, left // 128, lane)
            )
    b_act = split(act_of(conv[:, width : width + NST]))
    state[...] = fine(tn, (weighted[...], weighted_low[...]), b_act)


def conv_state(ends, idx, value, select, step, halo, params, micro_count, row_count):
    width = value.shape[1]
    heads = step.shape[1]
    total = micro_count * row_count
    return call(
        conv_body,
        (micro_count,),
        (ends, idx),
        [value, select, step, halo, params.taps, params.head_rows],
        [
            rows(row_count, width),
            rows(row_count, 2 * NST),
            rows(row_count, heads),
            rows(8, width + 2 * NST),
            whole((8, width + 2 * NST)),
            whole((8, 128)),
        ],
        [
            struct((total, width + 2 * NST)),
            struct((total, 128)),
            struct((micro_count * 128, row_count)),
            struct((micro_count * width, NST)),
        ],
        [
            rows(row_count, width + 2 * NST),
            rows(row_count, 128),
            rows(128, row_count),
            rows(width, NST),
        ],
        [
            pltpu.VMEM((row_count + 8, width + 2 * NST), F32),
            pltpu.VMEM((row_count, width), BF16),
            pltpu.VMEM((row_count, width), BF16),
        ],
        flops=40 * total * width,
    )


def mask_bias(ends, idx, micro, row_count):
    base = idx[0]
    seg_col = seg_at(base + lax.broadcasted_iota(jnp.int32, (row_count, 1), 0), ends, micro)
    seg_row = seg_at(base + lax.broadcasted_iota(jnp.int32, (1, row_count), 1), ends, micro)
    row_id = lax.broadcasted_iota(jnp.int32, (row_count, row_count), 0)
    col_id = lax.broadcasted_iota(jnp.int32, (row_count, row_count), 1)
    return jnp.where((seg_col == seg_row) & (row_id >= col_id), 0.0, -1e30)


def sides(values, lane):
    return (
        split(jnp.where(lane < P_SIZE, values, 0.0)),
        split(jnp.where(lane < P_SIZE, 0.0, values)),
    )


def scan_body(ends, idx, conv, table, table_t, skip, out, scores, bias):
    micro = pl.program_id(0)
    row_count = conv.shape[0]
    width = conv.shape[1] - 2 * NST
    half = row_count // 2
    b_act = split(act_of(conv[:, width : width + NST]))
    c_act = split(act_of(conv[:, width + NST :]))
    scores[...] = fine(nt, c_act, b_act)
    bias[...] = mask_bias(ends, idx, micro, row_count)
    lane = lax.broadcasted_iota(jnp.int32, (row_count, 128), 1)
    for pair in range(width // 128):
        span = slice(128 * pair, 128 * pair + 128)
        x_act = act_of(conv[:, span])
        halves = sides(x_act * pair_of(table[...], DT, pair, lane), lane)
        direct = skip[:, span] * x_act
        for top, bottom in ((0, half), (half, row_count)):
            result = direct[top:bottom, :]
            for side in range(2):
                head = 2 * pair + side
                cum_col = table[top:bottom, CUM + head : CUM + head + 1]
                cum_row = table_t[CUM + head : CUM + head + 1, 0:bottom]
                decay = jnp.exp(cum_col - cum_row + bias[top:bottom, 0:bottom])
                mixing = split(decay * scores[top:bottom, 0:bottom])
                result = result + fine(nn, mixing, [part[0:bottom, :] for part in halves[side]])
            out[top:bottom, span] = result


def scan_local(ends, idx, conv, table, table_t, params, micro_count, row_count):
    width = conv.shape[1] - 2 * NST
    return call(
        scan_body,
        (micro_count,),
        (ends, idx),
        [conv, table, table_t, params.skip],
        [rows(row_count, width + 2 * NST), rows(row_count, 128), rows(128, row_count), whole((1, width))],
        [struct((micro_count * row_count, width))],
        [rows(row_count, width)],
        [pltpu.VMEM((row_count, row_count), F32), pltpu.VMEM((row_count, row_count), F32)],
        flops=30 * micro_count * row_count * row_count * (width // P_SIZE),
    )[0]


def mix_body(idx, local, select, table, entering, gate, scan, gated, sums):
    row_count, width = local.shape
    c_act = split(act_of(select[:, NST:]))
    lane = lax.broadcasted_iota(jnp.int32, (row_count, 128), 1)
    squares = jnp.zeros((row_count, 128), F32)
    for pair in range(width // 128):
        span = slice(128 * pair, 128 * pair + 128)
        carried = fine(nt, c_act, split(entering[span, :]))
        value = local[:, span] + carried * pair_of(table[...], DECIN, pair, lane)
        scan[:, span] = value
        result = value * act_of(gate[:, span])
        gated[:, span] = result
        squares = squares + result * result
    sums[...] = nt(jnp.ones((8, 128), F32), squares, EXACT)


def gate_mix(idx, local, conv, table, entering, gate, micro_count, row_count):
    width = local.shape[1]
    total = micro_count * row_count
    select_block = pl.BlockSpec((row_count, 2 * NST), lambda m, *_: (m, width // (2 * NST)))
    return call(
        mix_body,
        (micro_count,),
        (idx,),
        [local, conv, table, entering, gate],
        [
            rows(row_count, width),
            select_block,
            rows(row_count, 128),
            rows(width, NST),
            rows(row_count, width),
        ],
        [struct((total, width)), struct((total, width)), struct((micro_count * 8, row_count))],
        [rows(row_count, width), rows(row_count, width), rows(8, row_count)],
        flops=6 * total * width * NST,
    )


def out_body(idx, gated, s0, s1, s2, s3, gain, w_out, scaled, inverse, *refs):
    chunks, (low, product) = (refs[:4], refs[4:])
    row_count, width = gated.shape
    chunk = row_count // 4
    squares = (s0[...] + s1[...]) + (s2[...] + s3[...])
    inverse[...] = jnp.broadcast_to(
        lax.rsqrt(squares / (H * P_SIZE) + EPSILON).T[:, 0:1], (row_count, 128)
    )
    inv = inverse[:, 0:1]
    for left in range(0, width, 128):
        span = slice(left, left + 128)
        rounded = (gated[:, span] * inv * gain[:, span]).astype(BF16)
        low[:, span] = rounded
        scaled[:, span] = rounded.astype(F32)
    for left in range(0, D, 512):
        product[:, left : left + 512] = nn(low[...], w_out[:, left : left + 512])
    for piece in range(4):
        place = pl.multiple_of((idx[1] ^ piece) * chunk, chunk)
        chunks[piece][...] = product[pl.ds(place, chunk), :]


def out_project(idx, gated, sums, weights, micro_count, row_count):
    width = gated.shape[1]
    total = micro_count * row_count
    chunk = row_count // 4
    return call(
        out_body,
        (micro_count,),
        (idx,),
        [gated, *sums, weights.gate_gain, weights.out],
        [rows(row_count, width)] + [rows(8, row_count)] * 4 + [whole((1, width)), whole((width, D))],
        [struct((total, width)), struct((total, 128))] + [struct((micro_count * chunk, D))] * 4,
        [rows(row_count, width), rows(row_count, 128)] + [rows(chunk, D)] * 4,
        [pltpu.VMEM((row_count, width), BF16), pltpu.VMEM((row_count, D), F32)],
        flops=2 * total * width * D,
    )


def gated_body(idx, *refs, from_parts):
    if from_parts:
        parts, refs = (refs[:4], refs[4:])
    else:
        grad, parts, refs = (refs[0], refs[1:5], refs[5:])
    gate, scan, inverse, select, table, gain, w_out = refs[:7]
    low_grad, grad_gate, grad_scan, state, gain_grad = refs[7:12]
    refs = refs[12:]
    if from_parts:
        full, refs = (refs[0], refs[1:])
    norms, carried, carried_low = refs
    row_count, width = gate.shape
    chunk = row_count // 4
    for piece in range(4):
        place = pl.ds(pl.multiple_of((idx[1] ^ piece) * chunk, chunk), chunk)
        if from_parts:
            values = parts[piece][:, 0:D]
            full[place, :] = values
            low_grad[place, :] = values.astype(BF16)
            norms[place, :] = parts[piece][:, D:]
        else:
            norms[place, :] = parts[piece][...]
    if not from_parts:
        low_grad[...] = grad[...]
    inv = inverse[:, 0:1]
    inner = norms[:, 0:1]
    c_act = split(act_of(select[:, NST:]))
    lane = lax.broadcasted_iota(jnp.int32, (row_count, 128), 1)
    gain_grad[...] = jnp.zeros_like(gain_grad)
    for pair in range(width // 128):
        span = slice(128 * pair, 128 * pair + 128)
        grad_scaled = nt(low_grad[...], w_out[span, :])
        gate_pre = gate[:, span]
        sig = sigmoid(gate_pre)
        act = gate_pre * sig
        out = scan[:, span]
        normal = out * act * inv
        gain_grad[0:1, span] = jnp.sum(grad_scaled * normal, axis=0, keepdims=True)
        grad_gated = inv * (grad_scaled * gain[:, span]) - normal * (inv * inner)
        grad_out = grad_gated * act
        grad_scan[:, span] = grad_out
        grad_gate[:, span] = (
            (grad_gated * out * (sig * (1.0 + gate_pre * (1.0 - sig)))).astype(BF16).astype(F32)
        )
        carried[:, span], carried_low[:, span] = split(
            grad_out * pair_of(table[...], DECIN, pair, lane)
        )
    state[...] = fine(tn, (carried[...], carried_low[...]), c_act)


def gated_back(idx, grad, parts, gate, scan, inverse, conv, table, weights, micro_count, row_count):
    width = gate.shape[1]
    total = micro_count * row_count
    chunk = row_count // 4
    from_parts = grad is None
    select_block = pl.BlockSpec((row_count, 2 * NST), lambda m, *_: (m, width // (2 * NST)))
    ins = ([] if from_parts else [grad]) + [
        *parts, gate, scan, inverse, conv, table, weights.gate_gain, weights.out
    ]
    in_specs = (
        ([] if from_parts else [rows(row_count, D)])
        + [rows(chunk, part.shape[1]) for part in parts]
        + [
            rows(row_count, width),
            rows(row_count, width),
            rows(row_count, 128),
            select_block,
            rows(row_count, 128),
            whole((1, width)),
            whole((width, D)),
        ]
    )
    outs = [
        struct((total, D), BF16),
        struct((total, width)),
        struct((total, width)),
        struct((micro_count * width, NST)),
        struct((micro_count * 8, width)),
    ]
    out_specs = [
        rows(row_count, D),
        rows(row_count, width),
        rows(row_count, width),
        rows(width, NST),
        rows(8, width),
    ]
    if from_parts:
        outs.append(struct((total, D)))
        out_specs.append(rows(row_count, D))
    return call(
        partial(gated_body, from_parts=from_parts),
        (micro_count,),
        (idx,),
        ins,
        in_specs,
        outs,
        out_specs,
        [
            pltpu.VMEM((row_count, PAD), F32),
            pltpu.VMEM((row_count, width), BF16),
            pltpu.VMEM((row_count, width), BF16),
        ],
        flops=2 * total * width * D,
    )


def scan_back_body(
    ends, idx, conv, table, table_t, grad, entering, skip,
    grad_x, grad_bc, grad_rows, skip_grad,
    scores, bias, grad_scores, row_sums, col_sums,
):
    micro = pl.program_id(0)
    row_count, width = grad.shape
    heads = width // P_SIZE
    half = row_count // 2
    b_act = split(act_of(conv[:, width : width + NST]))
    c_act = split(act_of(conv[:, width + NST :]))
    scores[...] = fine(nt, c_act, b_act)
    bias[...] = mask_bias(ends, idx, micro, row_count)
    grad_scores[...] = jnp.zeros_like(grad_scores)
    row_sums[...] = jnp.zeros_like(row_sums)
    lane = lax.broadcasted_iota(jnp.int32, (row_count, 128), 1)
    grad_c = jnp.zeros((row_count, NST), F32)
    cum_grad = jnp.zeros((heads, row_count), F32)
    step_grad = jnp.zeros((heads, row_count), F32)
    direct_sum = jnp.zeros((heads, row_count), F32)
    for pair in range(width // 128):
        span = slice(128 * pair, 128 * pair + 128)
        pre = conv[:, span]
        x_act = pre * sigmoid(pre)
        step_pair = pair_of(table[...], DT, pair, lane)
        x_step = split(x_act * step_pair)
        grad_out = grad[:, span]
        halves = sides(grad_out, lane)
        pulled = []
        for top, bottom in ((0, half), (half, row_count)):
            pulled_here = jnp.zeros((bottom, 128), F32)
            for side in range(2):
                head = 2 * pair + side
                cum_col = table[top:bottom, CUM + head : CUM + head + 1]
                cum_row = table_t[CUM + head : CUM + head + 1, 0:bottom]
                decay = jnp.exp(cum_col - cum_row + bias[top:bottom, 0:bottom])
                mixing = decay * scores[top:bottom, 0:bottom]
                grad_mix = fine(
                    nt, [part[top:bottom, :] for part in halves[side]], [part[0:bottom, :] for part in x_step]
                )
                grad_scores[top:bottom, 0:bottom] += grad_mix * decay
                turn = grad_mix * mixing
                row_sums[top:bottom, head : head + 1] = jnp.sum(turn, axis=1, keepdims=True)
                col_part = jnp.sum(turn, axis=0, keepdims=True)
                if top == 0:
                    col_sums[head : head + 1, 0:bottom] = col_part
                else:
                    col_sums[head : head + 1, 0:top] += col_part[:, 0:top]
                    col_sums[head : head + 1, top:bottom] = col_part[:, top:bottom]
                pulled_here = pulled_here + tn(mixing.astype(BF16), halves[side][0][top:bottom, :])
            pulled.append(pulled_here)
        grad_step_x = jnp.concatenate([pulled[0] + pulled[1][0:half, :], pulled[1][half:, :]], axis=0)
        grad_x[:, span] = grad_step_x * step_pair + grad_out * skip[:, span]
        step_grad = step_grad + head_sums(grad_step_x * x_act, pair, heads)
        direct_sum = direct_sum + head_sums(grad_out * x_act, pair, heads)
        decayed = grad_out * pair_of(table[...], DECIN, pair, lane)
        state = split(entering[span, :])
        cum_grad = cum_grad + head_sums(decayed * fine(nt, c_act, state), pair, heads)
        grad_c = grad_c + fine(nn, split(decayed), state)
    low_scores = split(grad_scores[...])
    grad_bc[:, 0:NST] = fine(tn, low_scores, c_act)
    grad_bc[:, NST:] = grad_c + fine(nn, low_scores, b_act)
    grad_rows[0:heads, :] = cum_grad + row_sums[...].T[0:heads, :] - col_sums[...]
    grad_rows[heads:, :] = step_grad
    skip_grad[...] = jnp.broadcast_to(jnp.sum(direct_sum, axis=1, keepdims=True), (heads, 128))


def scan_back(ends, idx, conv, table, table_t, grad, entering, params, micro_count, row_count):
    width = grad.shape[1]
    heads = width // P_SIZE
    total = micro_count * row_count
    square = pltpu.VMEM((row_count, row_count), F32)
    return call(
        scan_back_body,
        (micro_count,),
        (ends, idx),
        [conv, table, table_t, grad, entering, params.skip],
        [
            rows(row_count, width + 2 * NST),
            rows(row_count, 128),
            rows(128, row_count),
            rows(row_count, width),
            rows(width, NST),
            whole((1, width)),
        ],
        [
            struct((total, width)),
            struct((total, 2 * NST)),
            struct((micro_count * 2 * heads, row_count)),
            struct((micro_count * heads, 128)),
        ],
        [
            rows(row_count, width),
            rows(row_count, 2 * NST),
            rows(2 * heads, row_count),
            rows(heads, 128),
        ],
        [square, square, square, pltpu.VMEM((row_count, 128), F32), pltpu.VMEM((heads, row_count), F32)],
        flops=100 * total * row_count * heads,
    )


def finish_body(
    idx, conv, table, table_t, grad_x, grad_bc, grad_rows, later, entering, head_cols,
    grad_value, grad_select, grad_step, small, weighted, weighted_low,
):
    row_count, width = grad_x.shape
    heads = width // P_SIZE
    b_pre = conv[:, width : width + NST]
    b_sig = sigmoid(b_pre)
    b_act = split(b_pre * b_sig)
    lane = lax.broadcasted_iota(jnp.int32, (row_count, 128), 1)
    end_grad = jnp.zeros((heads, row_count), F32)
    for pair in range(width // 128):
        span = slice(128 * pair, 128 * pair + 128)
        pre = conv[:, span]
        sig = sigmoid(pre)
        x_act = pre * sig
        end_pair = pair_of(table[...], ENDW, pair, lane)
        reached = fine(nt, b_act, split(later[span, :]))
        end_grad = end_grad + head_sums(x_act * reached, pair, heads)
        weighted[:, span], weighted_low[:, span] = split(x_act * end_pair)
        grad_value[:, span] = (grad_x[:, span] + end_pair * reached) * (
            sig * (1.0 + pre * (1.0 - sig))
        )
    grad_b = grad_bc[:, 0:NST] + fine(nn, (weighted[...], weighted_low[...]), split(later[...]))
    grad_select[:, 0:NST] = grad_b * (b_sig * (1.0 + b_pre * (1.0 - b_sig)))
    c_pre = conv[:, width + NST :]
    c_sig = sigmoid(c_pre)
    grad_select[:, NST:] = grad_bc[:, NST:] * (c_sig * (1.0 + c_pre * (1.0 - c_sig)))

    crossing = (later[...] * entering[...]).reshape(heads, P_SIZE, NST)
    crossing = jnp.sum(jnp.sum(crossing, axis=1), axis=1, keepdims=True)
    end_weighted = end_grad * table_t[ENDW : ENDW + heads, :]
    last = jnp.sum(end_weighted, axis=1, keepdims=True) + crossing * table_t[
        DECIN : DECIN + heads, row_count - 1 : row_count
    ]
    place = lax.broadcasted_iota(jnp.int32, (heads, row_count), 1)
    cum_grad = grad_rows[0:heads, :] - end_weighted + jnp.where(place == row_count - 1, last, 0.0)
    row_id = lax.broadcasted_iota(jnp.int32, (row_count, row_count), 0)
    col_id = lax.broadcasted_iota(jnp.int32, (row_count, row_count), 1)
    grad_decay = nn(cum_grad, (row_id >= col_id).astype(F32), EXACT)
    step_grad = grad_rows[heads:, :] + end_grad * table_t[BASE : BASE + heads, :]
    grad_pre = (step_grad - grad_decay * jnp.exp(head_cols[:, 0:1])) * table_t[SIG : SIG + heads, :]
    small[...] = jnp.zeros_like(small)
    small[:, 0:1] = jnp.sum(grad_pre, axis=1, keepdims=True)
    small[:, 1:2] = jnp.sum(grad_decay * table_t[LOG : LOG + heads, :], axis=1, keepdims=True)
    padded = jnp.concatenate([grad_pre, jnp.zeros((128 - heads, row_count), F32)], axis=0)
    grad_step[...] = padded.T.astype(BF16).astype(F32)


def scan_finish(
    idx, conv, table, table_t, grad_x, grad_bc, grad_rows, later, entering, params, micro_count, row_count
):
    width = grad_x.shape[1]
    heads = width // P_SIZE
    total = micro_count * row_count
    return call(
        finish_body,
        (micro_count,),
        (idx,),
        [conv, table, table_t, grad_x, grad_bc, grad_rows, later, entering, params.head_cols],
        [
            rows(row_count, width + 2 * NST),
            rows(row_count, 128),
            rows(128, row_count),
            rows(row_count, width),
            rows(row_count, 2 * NST),
            rows(2 * heads, row_count),
            rows(width, NST),
            rows(width, NST),
            whole((heads, 128)),
        ],
        [
            struct((total, width)),
            struct((total, 2 * NST)),
            struct((total, 128)),
            struct((micro_count * heads, 128)),
        ],
        [rows(row_count, width), rows(row_count, 2 * NST), rows(row_count, 128), rows(heads, 128)],
        [pltpu.VMEM((row_count, width), BF16), pltpu.VMEM((row_count, width), BF16)],
        flops=60 * total * width,
    )


def taps_back(taps, own_grads, inputs, row_count, span, before, after, tap_grads):
    own = own_grads[0:row_count, span]
    tap_grads[4:5, span] = jnp.sum(own, axis=0, keepdims=True)
    tap_grads[3:4, span] = jnp.sum(own * inputs[8:, span], axis=0, keepdims=True)
    total = own * taps[3:4, span]
    for step in range(1, K):
        tap = K - 1 - step
        tap_grads[tap : tap + 1, span] = jnp.sum(
            own * (inputs[8 - step : 8 - step + row_count, span] * before[step - 1]),
            axis=0,
            keepdims=True,
        )
        total = total + taps[tap : tap + 1, span] * (
            own_grads[step : step + row_count, span] * after[step - 1]
        )
    return total.astype(BF16)


def near_masks(ends, idx, row_count):
    micro = pl.program_id(0)
    at = idx[0] + lax.broadcasted_iota(jnp.int32, (row_count, 1), 0)
    seg = seg_at(at, ends, micro)
    before = [(seg_at(at - step, ends, micro) == seg).astype(F32) for step in range(1, K)]
    after = [(seg_at(at + step, ends, micro) == seg).astype(F32) for step in range(1, K)]
    return (before, after)


def conv_back_body(
    ends, idx, grad_value, halo_value, value, halo_in, taps, gate_part, grad_step, w_value, w_step,
    low_value, tap_grads, c0, c1, c2, c3,
    grads, extended, low, product,
):
    row_count, width = grad_value.shape
    chunk = row_count // 4
    before, after = near_masks(ends, idx, row_count)
    grads[0:row_count, :] = grad_value[...]
    grads[row_count:, :] = halo_value[...]
    extended[0:8, :] = halo_in[...]
    extended[8:, :] = value[...]
    tap_grads[...] = jnp.zeros_like(tap_grads)
    for left in range(0, width, 128):
        span = slice(left, left + 128)
        rounded = taps_back(taps, grads, extended, row_count, span, before, after, tap_grads)
        low[:, span] = rounded
        low_value[:, span] = rounded.astype(F32)
    low_step = grad_step[:, 0 : w_step.shape[1]].astype(BF16)
    for left in range(0, D, 512):
        span = slice(left, left + 512)
        product[:, span] = (
            gate_part[:, span] + nt(low[...], w_value[span, :]) + nt(low_step, w_step[span, :])
        )
    for piece, target in enumerate((c0, c1, c2, c3)):
        place = pl.multiple_of((idx[1] ^ piece) * chunk, chunk)
        target[...] = product[pl.ds(place, chunk), :]


def conv_back(
    ends, idx, grad_value, halo_value, value, halo_in, gate_part, grad_step, params, weights, micro_count, row_count
):
    width = grad_value.shape[1]
    heads = weights.step.shape[1]
    total = micro_count * row_count
    chunk = row_count // 4
    return call(
        conv_back_body,
        (micro_count,),
        (ends, idx),
        [
            grad_value, halo_value, value, halo_in, params.taps, gate_part, grad_step, weights.value,
            weights.step,
        ],
        [
            rows(row_count, width),
            rows(8, width),
            rows(row_count, width),
            rows(8, width),
            whole((8, width)),
            rows(row_count, D),
            rows(row_count, 128),
            whole((D, width)),
            whole((D, heads)),
        ],
        [struct((total, width + 128)), struct((micro_count * 8, width))] + [struct((micro_count * chunk, D))] * 4,
        [rows(row_count, width), rows(8, width)] + [rows(chunk, D)] * 4,
        [
            pltpu.VMEM((row_count + 8, width), F32),
            pltpu.VMEM((row_count + 8, width), F32),
            pltpu.VMEM((row_count, width), BF16),
            pltpu.VMEM((row_count, D), F32),
        ],
        flops=2 * total * width * D,
    )


def select_back_body(
    ends, idx, s0, s1, s2, s3, halo, select, halo_in, taps, grad_step, kept,
    low_select, tap_grads, rest, grads, extended,
):
    del kept
    row_count, columns = select.shape
    before, after = near_masks(ends, idx, row_count)
    grads[0:row_count, :] = (s0[...] + s1[...]) + (s2[...] + s3[...])
    grads[row_count:, :] = halo[...]
    extended[0:8, :] = halo_in[...]
    extended[8:, :] = select[...]
    tap_grads[...] = jnp.zeros_like(tap_grads)
    for left in range(0, columns, 128):
        span = slice(left, left + 128)
        rounded = taps_back(taps, grads, extended, row_count, span, before, after, tap_grads)
        low_select[:, span] = rounded.astype(F32)
    part = columns // 4
    rest[:, part:] = grad_step[:, 0 : 128 - part]
    for head in range(4):

        @pl.when(idx[1] == head)
        def _():
            rest[:, 0:part] = low_select[:, head * part : (head + 1) * part]


def select_back(ends, idx, selects, halo, select, halo_in, grad_step, kept, params, micro_count, row_count):
    total, columns = select.shape
    width = kept.shape[1] - 128
    right = width // columns
    ins = [*selects, halo, select, halo_in, params.taps, grad_step, kept]
    outs = [
        struct((total, columns)),
        struct((micro_count * 8, columns)),
        struct((total, width + 128)),
    ]

    def guarded(*refs):
        @pl.when(refs[1][4] == 1)
        def _():
            select_back_body(*refs)

    return pl.pallas_call(
        guarded,
        grid_spec=pltpu.PrefetchScalarGridSpec(
            num_scalar_prefetch=2,
            grid=(micro_count,),
            in_specs=[rows(row_count, columns)] * 4
            + [
                rows(8, columns),
                rows(row_count, columns),
                pl.BlockSpec((8, columns), lambda m, *_: (m, right)),
                pl.BlockSpec((8, columns), lambda m, *_: (0, right)),
                rows(row_count, 128),
                pl.BlockSpec(memory_space=pl.ANY),
            ],
            out_specs=[
                rows(row_count, columns),
                rows(8, columns),
                pl.BlockSpec((row_count, 128), lambda m, *_: (m, width // 128)),
            ],
            scratch_shapes=[
                pltpu.VMEM((row_count + 8, columns), F32),
                pltpu.VMEM((row_count + 8, columns), F32),
            ],
        ),
        out_shape=outs,
        input_output_aliases={11: 2},
        compiler_params=pltpu.CompilerParams(vmem_limit_bytes=VMEM_BYTES),
        cost_estimate=pl.CostEstimate(flops=30 * total * columns, bytes_accessed=9 * total * columns * 4, transcendentals=0),
    )(ends, idx, *ins)


def weight_body(idx, split, split_other, kept, kept_other, far, own, *, flip):
    def product(a, b):
        return tn(b, a) if flip else tn(a, b)

    low = kept[...].astype(BF16)
    low_other = kept_other[...].astype(BF16)
    result = product(split[...], low) + product(split_other[...].astype(BF16), low_other)

    @pl.when(pl.program_id(0) == 0)
    def _():
        far[...] = result

    @pl.when(pl.program_id(0) == 1)
    def _():
        own[...] = result


def weight_grad(idx, split, split_other, kept, kept_other, flip):
    total, width = kept.shape
    block = split.shape[1] // 4
    shape = (width, block) if flip else (block, width)
    return call(
        partial(weight_body, flip=flip),
        (2,),
        (idx,),
        [split, split_other, kept, kept_other],
        [
            pl.BlockSpec((total, block), lambda b, idx: (0, idx[2] ^ (2 - 2 * b))),
            pl.BlockSpec((total, block), lambda b, idx: (0, b)),
            whole((total, width)),
            whole((total, width)),
        ],
        [struct(shape), struct(shape)],
        [whole(shape), whole(shape)],
        flops=8 * total * block * width,
    )


def join_body(idx, p0, p1, p2, p3, *refs):
    out = refs[-1]
    chunk = p0.shape[0]
    use_other = idx[3] == 1 if len(refs) > 1 else False

    def from_parts():
        for piece, part in enumerate((p0, p1, p2, p3)):
            out[pl.ds(pl.multiple_of((idx[1] ^ piece) * chunk, chunk), chunk), :] = part[...]

    if len(refs) == 1:
        from_parts()
    else:

        @pl.when(use_other)
        def _():
            out[...] = refs[0][...]

        pl.when(jnp.logical_not(use_other))(from_parts)


def join(idx, parts, other, micro_count, row_count):
    chunk = row_count // 4
    others = [] if other is None else [other]
    return call(
        join_body,
        (micro_count,),
        (idx,),
        [*parts, *others],
        [rows(chunk, D)] * 4 + [rows(row_count, D)] * len(others),
        [struct((micro_count * row_count, D))],
        [rows(row_count, D)],
    )[0]


def after(value, *others):
    return lax.optimization_barrier((value, *others))[0]


def shards(
    block_input,
    out_grad,
    lengths,
    norm_gain,
    gate_weight,
    value_weight,
    select_weight,
    step_weight,
    conv_value,
    conv_value_bias,
    conv_select,
    conv_select_bias,
    step_bias,
    log_rate,
    skip_gain,
    gate_gain,
    output_weight,
):
    micros, row_count, _ = block_input.shape
    total = micros * row_count
    width = gate_weight.shape[2]
    heads = width // P_SIZE
    chunk = row_count // 4
    tok_count = lax.axis_size(TOK)
    section, tok, head = (lax.axis_index(axis) for axis in AXES)
    ends = jnp.cumsum(lengths, axis=1).astype(jnp.int32)

    def scalars(flag, active):
        values = [tok * row_count, head, tok, flag, active]
        return jnp.stack([jnp.asarray(value, jnp.int32) for value in values])

    weights = SimpleNamespace(
        gain=norm_gain,
        gate=gate_weight[0],
        value=value_weight[0],
        select=select_weight[0],
        step=step_weight[0],
        out=output_weight[0],
        gate_gain=gate_gain[0].reshape(1, width),
    )
    taps = jnp.concatenate(
        [
            jnp.concatenate([conv_value[0].reshape(K, width), conv_select[0]], axis=1),
            jnp.concatenate([conv_value_bias[0].reshape(1, width), conv_select_bias], axis=1),
            jnp.zeros((3, width + 2 * NST), F32),
        ],
        axis=0,
    )
    params = SimpleNamespace(
        taps=taps,
        head_rows=jnp.pad(jnp.concatenate([step_bias, log_rate], axis=0), ((0, 6), (0, 128 - heads))),
        head_cols=jnp.pad(log_rate[0][:, None], ((0, 0), (0, 127))),
        skip=jnp.repeat(skip_gain[0], P_SIZE)[None, :],
    )

    def chunk_of(values):
        parts = values.reshape(micros, 4, chunk, values.shape[-1])
        mine = lax.dynamic_index_in_dim(parts, head, 1, keepdims=False)
        return mine.reshape(micros * chunk, values.shape[-1])

    def gather(values, layer):
        return [values] + [to_head(values, layer, step) for step in (1, 2, 3)]

    def reduce_chunks(parts, layer):
        moved = [to_head(parts[step], layer, step) for step in (1, 2, 3)]
        return (parts[0] + moved[0]) + (moved[1] + moved[2])

    def wave(layer, local, table, backward, ahead):
        decay = table.reshape(micros, row_count, 128)[:, row_count - 1, DECIN : DECIN + heads]
        shape = (micros, heads, P_SIZE, NST)
        entering = None
        for hop in range(tok_count - 1):
            leaving = local
            if entering is not None:
                leaving = (
                    local.reshape(shape) + decay[:, :, None, None] * entering.reshape(shape)
                ).reshape(local.shape)
            source = tok_count - 1 - hop if backward else hop
            target = source - 1 if backward else source + 1

            def move(t, h, source=source, target=target):
                return (target if t == source else -1, h)

            if hop in ahead:
                leaving = after(leaving, *ahead[hop])
            received = send(leaving, layer, move)
            entering = received if entering is None else entering + received
        return entering

    def forward(layer, parts, chunk_in):
        idx = scalars(0, section == layer)
        normed, value, select, step = in_project(idx, parts, weights, micros, row_count)
        edge = jnp.concatenate(
            [
                value.reshape(micros, row_count, width)[:, row_count - 8 :],
                select.reshape(micros, row_count, 2 * NST)[:, row_count - 8 :],
            ],
            axis=-1,
        ).reshape(micros * 8, width + 2 * NST)
        halo = to_tok(edge, layer, 1)
        conv, table, table_t, state = conv_state(
            ends, idx, value, select, step, halo, params, micros, row_count
        )
        gate = gate_project(idx, after(normed, state), weights.gate)
        local = scan_local(ends, idx, conv, table, table_t, params, micros, row_count)
        entering = wave(layer, state, table, False, {1: (gate, local)})
        scan, gated, sums = gate_mix(idx, local, conv, table, entering, gate, micros, row_count)
        scaled, inverse, *pieces = out_project(
            idx, gated, gather(sums, layer), weights, micros, row_count
        )
        branch = reduce_chunks(pieces, layer)
        saved = SimpleNamespace(
            normed=normed, gate=gate, value=value, select=select, halo=halo, conv=conv,
            table=table, table_t=table_t, entering=entering, scan=scan, inverse=inverse,
            scaled=scaled, branch=branch, chunk_in=chunk_in,
        )
        return (chunk_in + branch, saved)

    def norm_lanes(grad_chunk, branch):
        low = lax.reduce_precision(grad_chunk, 8, 7)
        inner = jnp.sum(low * branch, axis=-1, keepdims=True) / (H * P_SIZE)
        return jnp.broadcast_to(inner, (micros * chunk, PAD))

    def exchange(layer, values):
        return send(values, layer, lambda t, h: (t ^ 1, h))

    def split_blocks(values):
        block = values.shape[1] // 4
        return jnp.concatenate(
            [
                lax.dynamic_slice_in_dim(values, (tok ^ 3) * block, block, 1),
                lax.dynamic_slice_in_dim(values, (tok ^ 1) * block, block, 1),
            ],
            axis=1,
        ).astype(F32)

    def backward(layer, saved, grad, norm_parts, grad_chunk, pairs, shown, ahead, waits):
        idx = scalars(0, section == layer)
        low_grad, grad_gate, grad_scan, state, gain_grad, *full = gated_back(
            idx, grad, norm_parts, saved.gate, saved.scan, saved.inverse, saved.conv, saved.table,
            weights, micros, row_count,
        )
        grad_x, grad_bc, grad_rows, skip_grad = scan_back(
            ends, idx, saved.conv, saved.table, saved.table_t, grad_scan, saved.entering, params,
            micros, row_count,
        )
        gate_part = lax.dot_general(
            after(grad_gate, grad_bc).astype(BF16),
            weights.gate,
            (((1,), (1,)), ((), ())),
            preferred_element_type=F32,
        )
        pieces = shown(state)
        later = wave(
            layer,
            state,
            saved.table,
            True,
            {1: (grad_bc, *ahead[0], *pieces[1:2]), 2: (gate_part, *ahead[1], *pieces[2:3])},
        )
        later = after(later, *pieces[3:], *waits[0])
        grad_value, grad_select, grad_step, small = scan_finish(
            idx, saved.conv, saved.table, saved.table_t, grad_x, grad_bc, grad_rows, later,
            saved.entering, params, micros, row_count,
        )
        first_value = grad_value.reshape(micros, row_count, width)[:, :8].reshape(micros * 8, width)
        halo_value = to_tok(first_value, layer, -1)
        selects = gather(grad_select, layer)
        low_value, value_taps, *pieces = conv_back(
            ends, idx, grad_value, halo_value, saved.value, saved.halo, gate_part, grad_step, params,
            weights, micros, row_count,
        )
        kept = SimpleNamespace(scaled=saved.scaled, gate=grad_gate, low_grad=low_grad)
        products, first_needed = pairs(kept, halo_value)
        grad_normed = after(reduce_chunks(pieces, layer), *first_needed, *waits[1])
        first_select = sum(
            part.reshape(micros, row_count, 2 * NST)[:, :8].reshape(micros * 8, 2 * NST) for part in selects
        )
        halo_select = to_tok(first_select, layer, -1)
        low_select, select_taps, low_rest = select_back(
            ends, idx, selects, halo_select, saved.select, saved.halo, grad_step, low_value, params,
            micros, row_count,
        )
        grad_normed = grad_normed + lax.dot_general(
            chunk_of(low_select).astype(BF16),
            weights.select,
            (((1,), (1,)), ((), ())),
            preferred_element_type=F32,
        )
        hidden = saved.chunk_in
        inv = lax.rsqrt(jnp.mean(hidden * hidden, axis=-1, keepdims=True) + EPSILON)
        norm_grad = jnp.sum(grad_normed * hidden * inv, axis=0)
        weighted = grad_normed * weights.gain
        grad_hidden = (
            grad_chunk
            + inv * weighted
            - hidden * (inv * inv * inv) * jnp.mean(weighted * hidden, axis=-1, keepdims=True)
        )
        kept.value = low_rest
        sums = (
            norm_grad,
            jnp.concatenate(
                [
                    value_taps.reshape(micros, 8, -1)[:, : K + 1].sum(0).reshape(-1),
                    select_taps.reshape(micros, 8, -1)[:, : K + 1].sum(0).reshape(-1),
                    gain_grad.reshape(micros, 8, -1)[:, 0].sum(0),
                    small.reshape(micros, heads, 128).sum(0)[:, :2].T.reshape(-1),
                    skip_grad.reshape(micros, heads, 128).sum(0)[:, 0],
                ]
            ),
        )
        return (grad_hidden, kept, sums, full, products)

    def pair_product(layer, split, split_other, kept, flip, other):
        idx = scalars(0, section == layer)
        far, own = weight_grad(idx, split, split_other, kept, other, flip)
        return (own, send(far, layer, lambda t, h: (t ^ 2, h)))

    first = section == 0
    pairwise = tok_count == 4
    grad_rows_1 = out_grad.reshape(total, D)

    input_rows = block_input.reshape(total, D)
    chunk_0 = chunk_of(input_rows).astype(F32)
    out_0, saved_0 = forward(0, [input_rows], chunk_0)
    moved = out_0
    if pairwise:
        grad_other_1 = exchange(1, split_blocks(grad_rows_1))
        moved = after(out_0, grad_other_1)

    chunk_1 = lax.ppermute(moved, SECTION, [(0, 1)])
    parts_1 = gather(chunk_1, 1)
    if pairwise:
        other_0 = exchange(0, after(split_blocks(saved_0.normed), out_0))
        scaled_0 = exchange(0, after(saved_0.scaled, out_0))
        parts_1[0] = after(parts_1[0], other_0)
    out_1, saved_1 = forward(1, parts_1, chunk_1)

    grad_chunk_1 = chunk_of(grad_rows_1).astype(F32)
    lanes_1 = norm_lanes(grad_chunk_1, saved_1.branch)
    all_lanes_1 = gather(lanes_1, 1)
    if pairwise:
        other_1 = exchange(1, after(split_blocks(saved_1.normed), saved_1.entering))
        scaled_1 = exchange(1, saved_1.scaled)
        all_lanes_1[0] = after(all_lanes_1[0], other_1, scaled_0)

    def pairs_1(kept, done):
        if not pairwise:
            return ([], ())
        products = [
            pair_product(1, kept.low_grad, grad_other_1, kept.scaled, True, scaled_1),
            pair_product(1, saved_1.normed, other_1, kept.gate, False, exchange(1, after(kept.gate, done))),
        ]
        return (products, (products[0][0],))

    shown_1 = []

    def show_1(state):
        shown_1.extend(gather(after(out_1, state), 1))
        return shown_1

    grad_mid, kept_1, sums_1, _, big_1 = backward(
        1, saved_1, grad_rows_1, all_lanes_1, grad_chunk_1, pairs_1, show_1, ((scaled_1,) if pairwise else (), ()), ((), ())
    )
    full_1 = join(scalars(0, section == 1), parts_1, None, micros, row_count)
    layer_out = join(
        scalars(first, 1), shown_1, lax.ppermute(full_1, SECTION, [(1, 0)]), micros, row_count
    )
    if pairwise:
        big_1.append(
            pair_product(1, saved_1.normed, other_1, kept_1.value, False, exchange(1, kept_1.value))
        )

    grad_chunk_0 = lax.ppermute(grad_mid, SECTION, [(1, 0)])
    lanes_0 = norm_lanes(grad_chunk_0, saved_0.branch)
    payload = jnp.concatenate([grad_chunk_0, lanes_0], axis=1)

    def pairs_0(kept, done):
        if not pairwise:
            return ([], ())
        grad_other_0 = exchange(0, after(split_blocks(kept.low_grad), done))
        products = [
            pair_product(0, saved_0.normed, other_0, kept.gate, False, exchange(0, after(kept.gate, done))),
            pair_product(0, kept.low_grad, grad_other_0, kept.scaled, True, scaled_0),
        ]
        return (products, (products[0][0],))

    parts_0 = gather(payload, 0)
    ahead, waits = (((), ()), ((), ()))
    if pairwise:
        (_, scaled_far), (gate_own, gate_far), (value_own, value_far) = big_1
        parts_0[0] = after(parts_0[0], gate_own, scaled_far)
        ahead = ((value_own, gate_far), ())
        waits = ((), (value_far,))
    grad_in, kept_0, sums_0, (full_0,), big_0 = backward(
        0, saved_0, None, parts_0, grad_chunk_0, pairs_0, lambda state: [], ahead, waits
    )
    input_grad = join(
        scalars(section == 1, 1),
        gather(grad_in, 0),
        lax.ppermute(full_0, SECTION, [(0, 1)]),
        micros,
        row_count,
    )

    def chosen(left, right):
        return jnp.where(first, left, right)

    if pairwise:
        last = after(saved_0.normed, big_0[0][1])
        big_0.append(pair_product(0, last, other_0, kept_0.value, False, exchange(0, kept_0.value)))
        big_0[0], big_0[1] = (big_0[1], big_0[0])
        scaled_sum, gate_sum, value_sum = (
            chosen(own_0 + far_0, own_1 + far_1)
            for (own_0, far_0), (own_1, far_1) in zip(big_0, big_1, strict=True)
        )
    else:
        normed = chosen(saved_0.normed, saved_1.normed)

        def scattered(left, right, axis):
            return lax.psum_scatter(
                tn(left.astype(BF16), right.astype(BF16)), TOK, scatter_dimension=axis, tiled=True
            )

        scaled_sum = scattered(
            chosen(kept_0.scaled, kept_1.scaled), chosen(kept_0.low_grad, kept_1.low_grad), 1
        )
        gate_sum = scattered(normed, chosen(kept_0.gate, kept_1.gate), 0)
        value_sum = scattered(normed, chosen(kept_0.value, kept_1.value), 0)
    quarter = 2 * NST // 4
    select_sum = lax.all_gather(value_sum[:, width : width + quarter], HEAD, axis=1, tiled=True)

    def sum_over(values, axis):
        count = lax.axis_size(axis)
        if count != 4:
            return lax.psum(values, axis)
        moved = [
            lax.ppermute(values, axis, [(source, source ^ step) for source in range(count)])
            for step in (1, 2, 3)
        ]
        return (values + moved[0]) + (moved[1] + moved[2])

    norm_sum, head_sum = (chosen(left, right) for left, right in zip(sums_0, sums_1, strict=True))
    packed = sum_over(jnp.concatenate([norm_sum, head_sum]), TOK)
    norm_sum = sum_over(lax.dynamic_slice_in_dim(packed[:D], tok * (D // tok_count), D // tok_count, 0), HEAD)
    head_sum = packed[D:]
    pieces, place = ([], 0)
    for shape in ((K + 1, width), (K + 1, 2 * NST), (heads, P_SIZE), (heads,), (heads,), (heads,)):
        size = 1
        for extent in shape:
            size *= extent
        pieces.append(head_sum[place : place + size].reshape(shape))
        place += size
    value_taps, select_taps, gain_sum, bias_sum, rate_sum, skip_sum = pieces

    def mine(values, axis):
        size = values.shape[axis] // tok_count
        return lax.dynamic_slice_in_dim(values, tok * size, size, axis)

    outs = (
        layer_out.reshape(micros, row_count, D),
        input_grad.reshape(micros, row_count, D),
        norm_sum,
        gate_sum,
        value_sum[:, :width],
        select_sum,
        value_sum[:, width + quarter : width + quarter + heads],
        mine(value_taps[:K].reshape(K, heads, P_SIZE), 2),
        mine(value_taps[K].reshape(heads, P_SIZE), 1),
        mine(select_taps[:K], 1),
        mine(select_taps[K], 0),
        bias_sum,
        rate_sum,
        skip_sum,
        mine(gain_sum, 1),
        scaled_sum,
    )
    return tuple(value[None] for value in outs)


def solution(mesh):
    return jax.shard_map(
        shards,
        mesh=mesh,
        in_specs=(
            P(None, TOK, None),
            P(None, TOK, None),
            P(),
            P(SECTION, None),
            P(SECTION, None, HEAD),
            P(SECTION, None, HEAD),
            P(SECTION, None, None),
            P(SECTION, None, HEAD),
            P(SECTION, None, HEAD, None),
            P(SECTION, HEAD, None),
            P(SECTION, None, None),
            P(SECTION, None),
            P(SECTION, HEAD),
            P(SECTION, HEAD),
            P(SECTION, HEAD),
            P(SECTION, HEAD, None),
            P(SECTION, HEAD, None),
        ),
        out_specs=(
            P(SECTION, None, TOK, None),
            P(SECTION, None, TOK, None),
            P(SECTION, TOK),
            P(SECTION, TOK, HEAD),
            P(SECTION, TOK, HEAD),
            P(SECTION, TOK, None),
            P(SECTION, TOK, HEAD),
            P(SECTION, None, HEAD, TOK),
            P(SECTION, HEAD, TOK),
            P(SECTION, None, TOK),
            P(SECTION, TOK),
            P(SECTION, HEAD),
            P(SECTION, HEAD),
            P(SECTION, HEAD),
            P(SECTION, HEAD, TOK),
            P(SECTION, HEAD, TOK),
        ),
        check_vma=False,
    )
```

```python
from functools import partial
from types import SimpleNamespace

import jax
import jax.numpy as jnp
from jax import lax
from jax.experimental import pallas as pl
from jax.experimental.pallas import tpu as pltpu
from jax.sharding import PartitionSpec as P

D = 2048
H = 64
P_SIZE = 64
NST = 128
K = 4
EPSILON = 1e-05
SECTION, TOK, HEAD = AXES = ("section", "tok", "head")
F32 = jnp.float32
BF16 = jnp.bfloat16
EXACT = lax.Precision.HIGHEST
VMEM_BYTES = 58 * 1024 * 1024
PAD = 128

DT, CUM, SIG, LOG, ENDW, DECIN, BASE = (0, 16, 32, 48, 64, 80, 96)


def send(value, section, move):
    tok_count, head_count = (lax.axis_size(TOK), lax.axis_size(HEAD))

    def flat(tok, head):
        return (section * tok_count + tok) * head_count + head

    pairs = []
    for tok in range(tok_count):
        for head in range(head_count):
            target = move(tok, head)
            if 0 <= target[0] < tok_count:
                pairs.append((flat(tok, head), flat(*target)))
    return lax.ppermute(value, AXES, pairs)


def to_head(value, section, step):
    return send(value, section, lambda tok, head: (tok, head ^ step))


def to_tok(value, section, step):
    return send(value, section, lambda tok, head: (tok + step, head))


def nn(left, right, precision=None):
    return lax.dot_general(
        left, right, (((1,), (0,)), ((), ())), precision=precision, preferred_element_type=F32
    )


def nt(left, right, precision=None):
    return lax.dot_general(
        left, right, (((1,), (1,)), ((), ())), precision=precision, preferred_element_type=F32
    )


def tn(left, right):
    return lax.dot_general(left, right, (((0,), (0,)), ((), ())), preferred_element_type=F32)


def split(values):
    high = values.astype(BF16)
    return (high, (values - high.astype(F32)).astype(BF16))


def fine(product, left, right):
    return product(left[0], right[0]) + (product(left[0], right[1]) + product(left[1], right[0]))


def act_of(values):
    return values * sigmoid(values)


def sigmoid(values):
    return 1.0 / (1.0 + jnp.exp(-values))


def seg_at(points, ends, micro):
    inside = (points >= ends[micro, 0]).astype(jnp.int32)
    for which in range(1, 4):
        inside = inside + (points >= ends[micro, which]).astype(jnp.int32)
    return jnp.where(points >= 0, inside, -1)


def call(body, grid, scalars, ins, in_specs, outs, out_specs, scratch=(), flops=0, marks=()):
    flag = len(scalars) - 1
    read = len(scalars) + len(ins)

    def guarded(*refs):
        @pl.when(refs[flag][4] == 1)
        def _():
            body(*refs[:read], *refs[read + len(marks) :])

    moved = sum(a.size * a.dtype.itemsize for a in ins)
    moved += sum(o.size * o.dtype.itemsize for o in outs)
    return pl.pallas_call(
        guarded,
        grid_spec=pltpu.PrefetchScalarGridSpec(
            num_scalar_prefetch=len(scalars),
            grid=grid,
            in_specs=in_specs + [whole(mark.shape) for mark in marks],
            out_specs=out_specs,
            scratch_shapes=list(scratch),
        ),
        out_shape=outs,
        compiler_params=pltpu.CompilerParams(vmem_limit_bytes=VMEM_BYTES),
        cost_estimate=pl.CostEstimate(flops=flops, bytes_accessed=moved, transcendentals=0),
    )(*scalars, *ins, *marks)


def rows(count, width):
    return pl.BlockSpec((count, width), lambda m, *_: (m, 0))


def whole(shape):
    return pl.BlockSpec(shape, lambda m, *_: (0,) * len(shape))


def struct(shape, dtype=F32):
    return jax.ShapeDtypeStruct(shape, dtype)


def pair_of(table, base, pair, lane):
    first = table[:, base + 2 * pair : base + 2 * pair + 1]
    second = table[:, base + 2 * pair + 1 : base + 2 * pair + 2]
    return jnp.where(lane < P_SIZE, first, second)


def head_sums(values, pair, head_count):
    owner = lax.broadcasted_iota(jnp.int32, (head_count, 2 * P_SIZE), 0)
    lane = lax.broadcasted_iota(jnp.int32, (head_count, 2 * P_SIZE), 1)
    chosen = (owner == 2 * pair + (lane >= P_SIZE).astype(jnp.int32)).astype(BF16)
    high = values.astype(BF16)
    low = (values - high.astype(F32)).astype(BF16)
    return nt(chosen, high) + nt(chosen, low)


def in_body(idx, *refs, part_count, micro_count, row_count):
    parts, refs = (refs[:part_count], refs[part_count:])
    gain, w_value, w_select, w_step, normed, value, select, step = refs
    chunk = row_count // 4
    step_id = pl.program_id(0)

    @pl.when(step_id == 0)
    def _():
        for micro in range(micro_count):
            for piece in range(4):
                if part_count == 1:
                    place = micro * row_count + piece * chunk
                    values = parts[0][place : place + chunk, :].astype(F32)
                else:
                    place = pl.multiple_of(micro * row_count + (idx[1] ^ piece) * chunk, chunk)
                    values = parts[piece][micro * chunk : (micro + 1) * chunk, :]
                inv = lax.rsqrt(jnp.mean(values * values, axis=-1, keepdims=True) + EPSILON)
                normed[pl.ds(place, chunk), :] = (values * inv * gain[...]).astype(BF16)
        select[...] = nn(normed[...], w_select[...])
        step[...] = nn(normed[...], w_step[...])

    value[...] = nn(normed[...], w_value[...])


def in_project(idx, parts, weights, micro_count, row_count):
    total = micro_count * row_count
    width = weights.value.shape[1]
    heads = weights.step.shape[1]
    tile = width // 4
    outs = [
        struct((total, D), BF16),
        struct((total, width)),
        struct((total, 2 * NST)),
        struct((total, heads)),
    ]
    cols = pl.BlockSpec((total, tile), lambda j, *_: (0, j))
    wcols = pl.BlockSpec((D, tile), lambda j, *_: (0, j))
    return call(
        partial(in_body, part_count=len(parts), micro_count=micro_count, row_count=row_count),
        (4,),
        (idx,),
        [*parts, weights.gain, weights.value, weights.select, weights.step],
        [whole(part.shape) for part in parts]
        + [whole((1, D)), wcols, whole((D, 2 * NST)), whole((D, heads))],
        outs,
        [whole((total, D)), cols, whole((total, 2 * NST)), whole((total, heads))],
        flops=2 * total * D * (width + 2 * NST),
    )


def gate_body(idx, normed, w_gate, gate):
    gate[...] = nn(normed[...], w_gate[...])


def gate_project(idx, normed, w_gate):
    total, width = (normed.shape[0], w_gate.shape[1])
    tile = width // 4
    return call(
        gate_body,
        (4,),
        (idx,),
        [normed, w_gate],
        [whole((total, D)), pl.BlockSpec((D, tile), lambda j, *_: (0, j))],
        [struct((total, width))],
        [pl.BlockSpec((total, tile), lambda j, *_: (0, j))],
        flops=2 * total * D * width,
    )[0]


def conv_body(
    ends, idx, value, select, step, halo, taps, head_rows,
    conv, table, table_t, state, extended, weighted, weighted_low,
):
    micro = pl.program_id(0)
    row_count, width = value.shape
    heads = step.shape[1]
    base = idx[0]
    at = base + lax.broadcasted_iota(jnp.int32, (row_count, 1), 0)
    seg = seg_at(at, ends, micro)
    seg_before = seg_at(base - 1 + jnp.zeros((1, 1), jnp.int32), ends, micro)
    seg_last = seg_at(base + row_count - 1 + jnp.zeros((1, 1), jnp.int32), ends, micro)
    carry = (seg == seg_before).astype(F32)
    tail = (seg == seg_last).astype(F32)

    pre = step[...] + head_rows[0:1, 0:heads]
    step_size = jnp.maximum(pre, 0.0) + jnp.log1p(jnp.exp(-jnp.abs(pre)))
    log_decay = -jnp.exp(head_rows[1:2, 0:heads]) * step_size
    row_id = lax.broadcasted_iota(jnp.int32, (row_count, row_count), 0)
    col_id = lax.broadcasted_iota(jnp.int32, (row_count, row_count), 1)
    cum = nn((row_id >= col_id).astype(F32), log_decay, EXACT)
    end_base = jnp.exp(cum[row_count - 1 : row_count, :] - cum) * tail
    decay_in = jnp.exp(cum) * carry
    table[...] = jnp.zeros_like(table)
    for place, part in (
        (DT, step_size),
        (CUM, cum),
        (SIG, sigmoid(pre)),
        (LOG, log_decay),
        (ENDW, end_base * step_size),
        (DECIN, decay_in),
        (BASE, end_base),
    ):
        table[:, place : place + heads] = part
    table_t[...] = table[...].T

    extended[0:8, :] = halo[...]
    extended[8:, 0:width] = value[...]
    extended[8:, width:] = select[...]
    masks = [(seg_at(at - (K - 1 - tap), ends, micro) == seg).astype(F32) for tap in range(K - 1)]
    lane = lax.broadcasted_iota(jnp.int32, (row_count, 128), 1)
    columns = width + 2 * NST
    for left in range(0, columns, 128):
        span = slice(left, left + 128)
        total = taps[4:5, span] + taps[3:4, span] * extended[8 : 8 + row_count, span]
        for tap in range(K - 1):
            total = total + taps[tap : tap + 1, span] * (
                extended[5 + tap : 5 + tap + row_count, span] * masks[tap]
            )
        conv[:, span] = total
        if left < width:
            weighted[:, span], weighted_low[:, span] = split(
                act_of(total) * pair_of(table[...], ENDW, left // 128, lane)
            )
    b_act = split(act_of(conv[:, width : width + NST]))
    state[...] = fine(tn, (weighted[...], weighted_low[...]), b_act)


def conv_state(ends, idx, value, select, step, halo, params, micro_count, row_count):
    width = value.shape[1]
    heads = step.shape[1]
    total = micro_count * row_count
    return call(
        conv_body,
        (micro_count,),
        (ends, idx),
        [value, select, step, halo, params.taps, params.head_rows],
        [
            rows(row_count, width),
            rows(row_count, 2 * NST),
            rows(row_count, heads),
            rows(8, width + 2 * NST),
            whole((8, width + 2 * NST)),
            whole((8, 128)),
        ],
        [
            struct((total, width + 2 * NST)),
            struct((total, 128)),
            struct((micro_count * 128, row_count)),
            struct((micro_count * width, NST)),
        ],
        [
            rows(row_count, width + 2 * NST),
            rows(row_count, 128),
            rows(128, row_count),
            rows(width, NST),
        ],
        [
            pltpu.VMEM((row_count + 8, width + 2 * NST), F32),
            pltpu.VMEM((row_count, width), BF16),
            pltpu.VMEM((row_count, width), BF16),
        ],
        flops=40 * total * width,
    )


def mask_bias(ends, idx, micro, row_count):
    base = idx[0]
    seg_col = seg_at(base + lax.broadcasted_iota(jnp.int32, (row_count, 1), 0), ends, micro)
    seg_row = seg_at(base + lax.broadcasted_iota(jnp.int32, (1, row_count), 1), ends, micro)
    row_id = lax.broadcasted_iota(jnp.int32, (row_count, row_count), 0)
    col_id = lax.broadcasted_iota(jnp.int32, (row_count, row_count), 1)
    return jnp.where((seg_col == seg_row) & (row_id >= col_id), 0.0, -1e30)


def sides(values, lane):
    return (
        split(jnp.where(lane < P_SIZE, values, 0.0)),
        split(jnp.where(lane < P_SIZE, 0.0, values)),
    )


def scan_body(ends, idx, conv, table, table_t, skip, out, scores, bias):
    micro = pl.program_id(0)
    row_count = conv.shape[0]
    width = conv.shape[1] - 2 * NST
    half = row_count // 2
    b_act = split(act_of(conv[:, width : width + NST]))
    c_act = split(act_of(conv[:, width + NST :]))
    scores[...] = fine(nt, c_act, b_act)
    bias[...] = mask_bias(ends, idx, micro, row_count)
    lane = lax.broadcasted_iota(jnp.int32, (row_count, 128), 1)
    for pair in range(width // 128):
        span = slice(128 * pair, 128 * pair + 128)
        x_act = act_of(conv[:, span])
        halves = sides(x_act * pair_of(table[...], DT, pair, lane), lane)
        direct = skip[:, span] * x_act
        for top, bottom in ((0, half), (half, row_count)):
            result = direct[top:bottom, :]
            for side in range(2):
                head = 2 * pair + side
                cum_col = table[top:bottom, CUM + head : CUM + head + 1]
                cum_row = table_t[CUM + head : CUM + head + 1, 0:bottom]
                decay = jnp.exp(cum_col - cum_row + bias[top:bottom, 0:bottom])
                mixing = split(decay * scores[top:bottom, 0:bottom])
                result = result + fine(nn, mixing, [part[0:bottom, :] for part in halves[side]])
            out[top:bottom, span] = result


def scan_local(ends, idx, conv, table, table_t, params, micro_count, row_count):
    width = conv.shape[1] - 2 * NST
    return call(
        scan_body,
        (micro_count,),
        (ends, idx),
        [conv, table, table_t, params.skip],
        [rows(row_count, width + 2 * NST), rows(row_count, 128), rows(128, row_count), whole((1, width))],
        [struct((micro_count * row_count, width))],
        [rows(row_count, width)],
        [pltpu.VMEM((row_count, row_count), F32), pltpu.VMEM((row_count, row_count), F32)],
        flops=30 * micro_count * row_count * row_count * (width // P_SIZE),
    )[0]


def mix_body(idx, local, select, table, entering, gate, *refs):
    grads, (scan, gated, sums) = (refs[:-3], refs[-3:])
    row_count, width = local.shape
    c_act = split(act_of(select[:, NST:]))
    lane = lax.broadcasted_iota(jnp.int32, (row_count, 128), 1)
    squares = jnp.zeros((row_count, 128), F32)
    inner = jnp.zeros((row_count, 128), F32)
    for pair in range(width // 128):
        span = slice(128 * pair, 128 * pair + 128)
        carried = fine(nt, c_act, split(entering[span, :]))
        value = local[:, span] + carried * pair_of(table[...], DECIN, pair, lane)
        scan[:, span] = value
        result = value * act_of(gate[:, span])
        gated[:, span] = result
        squares = squares + result * result
        if grads:
            inner = inner + result * (grads[0][:, span] * grads[1][:, span])
    ones = jnp.ones((4, 128), F32)
    sums[0:4, :] = nt(ones, squares, EXACT)
    sums[4:8, :] = nt(ones, inner, EXACT)


def gate_mix(idx, local, conv, table, entering, gate, grads, micro_count, row_count):
    width = local.shape[1]
    total = micro_count * row_count
    select_block = pl.BlockSpec((row_count, 2 * NST), lambda m, *_: (m, width // (2 * NST)))
    return call(
        mix_body,
        (micro_count,),
        (idx,),
        [local, conv, table, entering, gate, *grads],
        [
            rows(row_count, width),
            select_block,
            rows(row_count, 128),
            rows(width, NST),
            rows(row_count, width),
        ]
        + ([rows(row_count, width), whole((1, width))] if grads else []),
        [struct((total, width)), struct((total, width)), struct((micro_count * 8, row_count))],
        [rows(row_count, width), rows(row_count, width), rows(8, row_count)],
        flops=6 * total * width * NST,
    )


def back_body(idx, grad, w_out, out):
    out[...] = nt(grad[...], w_out[...])


def back_project(idx, grad, w_out, micro_count, row_count):
    total, width = (grad.shape[0], w_out.shape[0])
    tile = width // 4
    return call(
        back_body,
        (4,),
        (idx,),
        [grad, w_out],
        [whole((total, D)), pl.BlockSpec((tile, D), lambda j, *_: (j, 0))],
        [struct((total, width))],
        [pl.BlockSpec((total, tile), lambda j, *_: (0, j))],
        flops=2 * total * width * D,
    )[0]


def norms_of(sums):
    total = ((sums[0][...] + sums[1][...]) + (sums[2][...] + sums[3][...])) / (H * P_SIZE)
    total = total.T
    inv = lax.rsqrt(total[:, 0:1] + EPSILON)
    return (inv, total[:, 4:5] * inv)


def out_body(idx, gated, s0, s1, s2, s3, gain, w_out, scaled, *refs):
    chunks, (low, product) = (refs[:4], refs[4:])
    row_count, width = gated.shape
    chunk = row_count // 4
    inv, _ = norms_of((s0, s1, s2, s3))
    for left in range(0, width, 128):
        span = slice(left, left + 128)
        rounded = (gated[:, span] * inv * gain[:, span]).astype(BF16)
        low[:, span] = rounded
        scaled[:, span] = rounded.astype(F32)
    for left in range(0, D, 512):
        product[:, left : left + 512] = nn(low[...], w_out[:, left : left + 512])
    for piece in range(4):
        place = pl.multiple_of((idx[1] ^ piece) * chunk, chunk)
        chunks[piece][...] = product[pl.ds(place, chunk), :]


def out_project(idx, gated, sums, weights, micro_count, row_count, marks=()):
    width = gated.shape[1]
    total = micro_count * row_count
    chunk = row_count // 4
    return call(
        out_body,
        (micro_count,),
        (idx,),
        [gated, *sums, weights.gate_gain, weights.out],
        [rows(row_count, width)] + [rows(8, row_count)] * 4 + [whole((1, width)), whole((width, D))],
        [struct((total, width))] + [struct((micro_count * chunk, D))] * 4,
        [rows(row_count, width)] + [rows(chunk, D)] * 4,
        [pltpu.VMEM((row_count, width), BF16), pltpu.VMEM((row_count, D), F32)],
        flops=2 * total * width * D,
        marks=marks,
    )


def gated_body(idx, *refs, from_parts):
    sums, (gate, scan, select, table, gain), refs = (refs[:4], refs[4:9], refs[9:])
    if from_parts:
        parts, w_out, refs = (refs[:4], refs[4], refs[5:])
    else:
        grads, refs = (refs[0], refs[1:])
    grad_gate, grad_scan, state, gain_grad = refs[:4]
    if from_parts:
        low_grad, full, norms = refs[4:7]
    else:
        scaled = refs[4]
    carried, carried_low = refs[-2:]
    row_count, width = gate.shape
    chunk = row_count // 4
    inv, inner = norms_of(sums)
    if from_parts:
        for piece in range(4):
            place = pl.ds(pl.multiple_of((idx[1] ^ piece) * chunk, chunk), chunk)
            values = parts[piece][:, 0:D]
            full[place, :] = values
            low_grad[place, :] = values.astype(BF16)
            norms[place, :] = parts[piece][:, D:]
        inner = norms[:, 0:1]
    c_act = split(act_of(select[:, NST:]))
    lane = lax.broadcasted_iota(jnp.int32, (row_count, 128), 1)
    gain_grad[...] = jnp.zeros_like(gain_grad)
    for pair in range(width // 128):
        span = slice(128 * pair, 128 * pair + 128)
        grad_scaled = nt(low_grad[...], w_out[span, :]) if from_parts else grads[:, span]
        gate_pre = gate[:, span]
        sig = sigmoid(gate_pre)
        act = gate_pre * sig
        out = scan[:, span]
        normal = out * act * inv
        gain_grad[0:1, span] = jnp.sum(grad_scaled * normal, axis=0, keepdims=True)
        if not from_parts:
            scaled[:, span] = (normal * gain[:, span]).astype(BF16).astype(F32)
        grad_gated = inv * (grad_scaled * gain[:, span]) - normal * (inv * inner)
        grad_out = grad_gated * act
        grad_scan[:, span] = grad_out
        grad_gate[:, span] = (
            (grad_gated * out * (sig * (1.0 + gate_pre * (1.0 - sig)))).astype(BF16).astype(F32)
        )
        carried[:, span], carried_low[:, span] = split(
            grad_out * pair_of(table[...], DECIN, pair, lane)
        )
    state[...] = fine(tn, (carried[...], carried_low[...]), c_act)


def gated_back(idx, grads, parts, sums, gate, scan, conv, table, weights, micro_count, row_count):
    width = gate.shape[1]
    total = micro_count * row_count
    chunk = row_count // 4
    from_parts = grads is None
    select_block = pl.BlockSpec((row_count, 2 * NST), lambda m, *_: (m, width // (2 * NST)))
    ins = [*sums, gate, scan, conv, table, weights.gate_gain]
    in_specs = [rows(8, row_count)] * 4 + [
        rows(row_count, width),
        rows(row_count, width),
        select_block,
        rows(row_count, 128),
        whole((1, width)),
    ]
    outs = [
        struct((total, width)),
        struct((total, width)),
        struct((micro_count * width, NST)),
        struct((micro_count * 8, width)),
    ]
    out_specs = [rows(row_count, width), rows(row_count, width), rows(width, NST), rows(8, width)]
    scratch = [pltpu.VMEM((row_count, width), BF16), pltpu.VMEM((row_count, width), BF16)]
    if from_parts:
        ins += [*parts, weights.out]
        in_specs += [rows(chunk, D + PAD)] * 4 + [whole((width, D))]
        outs += [struct((total, D), BF16), struct((total, D))]
        out_specs += [rows(row_count, D), rows(row_count, D)]
        scratch = [pltpu.VMEM((row_count, PAD), F32)] + scratch
    else:
        ins.append(grads)
        in_specs.append(rows(row_count, width))
        outs.append(struct((total, width)))
        out_specs.append(rows(row_count, width))
    return call(
        partial(gated_body, from_parts=from_parts),
        (micro_count,),
        (idx,),
        ins,
        in_specs,
        outs,
        out_specs,
        scratch,
        flops=2 * total * width * (D if from_parts else NST),
    )


def scan_back_body(
    ends, idx, conv, table, table_t, grad, entering, skip,
    grad_x, grad_bc, grad_rows, skip_grad,
    scores, bias, grad_scores, row_sums, col_sums,
):
    micro = pl.program_id(0)
    row_count, width = grad.shape
    heads = width // P_SIZE
    half = row_count // 2
    b_act = split(act_of(conv[:, width : width + NST]))
    c_act = split(act_of(conv[:, width + NST :]))
    scores[...] = fine(nt, c_act, b_act)
    bias[...] = mask_bias(ends, idx, micro, row_count)
    grad_scores[...] = jnp.zeros_like(grad_scores)
    row_sums[...] = jnp.zeros_like(row_sums)
    lane = lax.broadcasted_iota(jnp.int32, (row_count, 128), 1)
    grad_c = jnp.zeros((row_count, NST), F32)
    cum_grad = jnp.zeros((heads, row_count), F32)
    step_grad = jnp.zeros((heads, row_count), F32)
    direct_sum = jnp.zeros((heads, row_count), F32)
    for pair in range(width // 128):
        span = slice(128 * pair, 128 * pair + 128)
        pre = conv[:, span]
        x_act = pre * sigmoid(pre)
        step_pair = pair_of(table[...], DT, pair, lane)
        x_step = split(x_act * step_pair)
        grad_out = grad[:, span]
        halves = sides(grad_out, lane)
        pulled = []
        for top, bottom in ((0, half), (half, row_count)):
            pulled_here = jnp.zeros((bottom, 128), F32)
            for side in range(2):
                head = 2 * pair + side
                cum_col = table[top:bottom, CUM + head : CUM + head + 1]
                cum_row = table_t[CUM + head : CUM + head + 1, 0:bottom]
                decay = jnp.exp(cum_col - cum_row + bias[top:bottom, 0:bottom])
                mixing = decay * scores[top:bottom, 0:bottom]
                grad_mix = fine(
                    nt, [part[top:bottom, :] for part in halves[side]], [part[0:bottom, :] for part in x_step]
                )
                grad_scores[top:bottom, 0:bottom] += grad_mix * decay
                turn = grad_mix * mixing
                row_sums[top:bottom, head : head + 1] = jnp.sum(turn, axis=1, keepdims=True)
                col_part = jnp.sum(turn, axis=0, keepdims=True)
                if top == 0:
                    col_sums[head : head + 1, 0:bottom] = col_part
                else:
                    col_sums[head : head + 1, 0:top] += col_part[:, 0:top]
                    col_sums[head : head + 1, top:bottom] = col_part[:, top:bottom]
                pulled_here = pulled_here + tn(mixing.astype(BF16), halves[side][0][top:bottom, :])
            pulled.append(pulled_here)
        grad_step_x = jnp.concatenate([pulled[0] + pulled[1][0:half, :], pulled[1][half:, :]], axis=0)
        grad_x[:, span] = grad_step_x * step_pair + grad_out * skip[:, span]
        step_grad = step_grad + head_sums(grad_step_x * x_act, pair, heads)
        direct_sum = direct_sum + head_sums(grad_out * x_act, pair, heads)
        decayed = grad_out * pair_of(table[...], DECIN, pair, lane)
        state = split(entering[span, :])
        cum_grad = cum_grad + head_sums(decayed * fine(nt, c_act, state), pair, heads)
        grad_c = grad_c + fine(nn, split(decayed), state)
    low_scores = split(grad_scores[...])
    grad_bc[:, 0:NST] = fine(tn, low_scores, c_act)
    grad_bc[:, NST:] = grad_c + fine(nn, low_scores, b_act)
    grad_rows[0:heads, :] = cum_grad + row_sums[...].T[0:heads, :] - col_sums[...]
    grad_rows[heads:, :] = step_grad
    skip_grad[...] = jnp.broadcast_to(jnp.sum(direct_sum, axis=1, keepdims=True), (heads, 128))


def scan_back(ends, idx, conv, table, table_t, grad, entering, params, micro_count, row_count):
    width = grad.shape[1]
    heads = width // P_SIZE
    total = micro_count * row_count
    square = pltpu.VMEM((row_count, row_count), F32)
    return call(
        scan_back_body,
        (micro_count,),
        (ends, idx),
        [conv, table, table_t, grad, entering, params.skip],
        [
            rows(row_count, width + 2 * NST),
            rows(row_count, 128),
            rows(128, row_count),
            rows(row_count, width),
            rows(width, NST),
            whole((1, width)),
        ],
        [
            struct((total, width)),
            struct((total, 2 * NST)),
            struct((micro_count * 2 * heads, row_count)),
            struct((micro_count * heads, 128)),
        ],
        [
            rows(row_count, width),
            rows(row_count, 2 * NST),
            rows(2 * heads, row_count),
            rows(heads, 128),
        ],
        [square, square, square, pltpu.VMEM((row_count, 128), F32), pltpu.VMEM((heads, row_count), F32)],
        flops=100 * total * row_count * heads,
    )


def finish_body(
    idx, conv, table, table_t, grad_x, grad_bc, grad_rows, later, entering, head_cols,
    grad_value, grad_select, grad_step, small, weighted, weighted_low,
):
    row_count, width = grad_x.shape
    heads = width // P_SIZE
    b_pre = conv[:, width : width + NST]
    b_sig = sigmoid(b_pre)
    b_act = split(b_pre * b_sig)
    lane = lax.broadcasted_iota(jnp.int32, (row_count, 128), 1)
    end_grad = jnp.zeros((heads, row_count), F32)
    for pair in range(width // 128):
        span = slice(128 * pair, 128 * pair + 128)
        pre = conv[:, span]
        sig = sigmoid(pre)
        x_act = pre * sig
        end_pair = pair_of(table[...], ENDW, pair, lane)
        reached = fine(nt, b_act, split(later[span, :]))
        end_grad = end_grad + head_sums(x_act * reached, pair, heads)
        weighted[:, span], weighted_low[:, span] = split(x_act * end_pair)
        grad_value[:, span] = (grad_x[:, span] + end_pair * reached) * (
            sig * (1.0 + pre * (1.0 - sig))
        )
    grad_b = grad_bc[:, 0:NST] + fine(nn, (weighted[...], weighted_low[...]), split(later[...]))
    grad_select[:, 0:NST] = grad_b * (b_sig * (1.0 + b_pre * (1.0 - b_sig)))
    c_pre = conv[:, width + NST :]
    c_sig = sigmoid(c_pre)
    grad_select[:, NST:] = grad_bc[:, NST:] * (c_sig * (1.0 + c_pre * (1.0 - c_sig)))

    crossing = (later[...] * entering[...]).reshape(heads, P_SIZE, NST)
    crossing = jnp.sum(jnp.sum(crossing, axis=1), axis=1, keepdims=True)
    end_weighted = end_grad * table_t[ENDW : ENDW + heads, :]
    last = jnp.sum(end_weighted, axis=1, keepdims=True) + crossing * table_t[
        DECIN : DECIN + heads, row_count - 1 : row_count
    ]
    place = lax.broadcasted_iota(jnp.int32, (heads, row_count), 1)
    cum_grad = grad_rows[0:heads, :] - end_weighted + jnp.where(place == row_count - 1, last, 0.0)
    row_id = lax.broadcasted_iota(jnp.int32, (row_count, row_count), 0)
    col_id = lax.broadcasted_iota(jnp.int32, (row_count, row_count), 1)
    grad_decay = nn(cum_grad, (row_id >= col_id).astype(F32), EXACT)
    step_grad = grad_rows[heads:, :] + end_grad * table_t[BASE : BASE + heads, :]
    grad_pre = (step_grad - grad_decay * jnp.exp(head_cols[:, 0:1])) * table_t[SIG : SIG + heads, :]
    small[...] = jnp.zeros_like(small)
    small[:, 0:1] = jnp.sum(grad_pre, axis=1, keepdims=True)
    small[:, 1:2] = jnp.sum(grad_decay * table_t[LOG : LOG + heads, :], axis=1, keepdims=True)
    padded = jnp.concatenate([grad_pre, jnp.zeros((128 - heads, row_count), F32)], axis=0)
    grad_step[...] = padded.T.astype(BF16).astype(F32)


def scan_finish(
    idx, conv, table, table_t, grad_x, grad_bc, grad_rows, later, entering, params, micro_count, row_count
):
    width = grad_x.shape[1]
    heads = width // P_SIZE
    total = micro_count * row_count
    return call(
        finish_body,
        (micro_count,),
        (idx,),
        [conv, table, table_t, grad_x, grad_bc, grad_rows, later, entering, params.head_cols],
        [
            rows(row_count, width + 2 * NST),
            rows(row_count, 128),
            rows(128, row_count),
            rows(row_count, width),
            rows(row_count, 2 * NST),
            rows(2 * heads, row_count),
            rows(width, NST),
            rows(width, NST),
            whole((heads, 128)),
        ],
        [
            struct((total, width)),
            struct((total, 2 * NST)),
            struct((total, 128)),
            struct((micro_count * heads, 128)),
        ],
        [rows(row_count, width), rows(row_count, 2 * NST), rows(row_count, 128), rows(heads, 128)],
        [pltpu.VMEM((row_count, width), BF16), pltpu.VMEM((row_count, width), BF16)],
        flops=60 * total * width,
    )


def taps_back(taps, own_grads, inputs, row_count, span, before, after, tap_grads):
    own = own_grads[0:row_count, span]
    tap_grads[4:5, span] = jnp.sum(own, axis=0, keepdims=True)
    tap_grads[3:4, span] = jnp.sum(own * inputs[8:, span], axis=0, keepdims=True)
    total = own * taps[3:4, span]
    for step in range(1, K):
        tap = K - 1 - step
        tap_grads[tap : tap + 1, span] = jnp.sum(
            own * (inputs[8 - step : 8 - step + row_count, span] * before[step - 1]),
            axis=0,
            keepdims=True,
        )
        total = total + taps[tap : tap + 1, span] * (
            own_grads[step : step + row_count, span] * after[step - 1]
        )
    return total.astype(BF16)


def near_masks(ends, idx, row_count):
    micro = pl.program_id(0)
    at = idx[0] + lax.broadcasted_iota(jnp.int32, (row_count, 1), 0)
    seg = seg_at(at, ends, micro)
    before = [(seg_at(at - step, ends, micro) == seg).astype(F32) for step in range(1, K)]
    after = [(seg_at(at + step, ends, micro) == seg).astype(F32) for step in range(1, K)]
    return (before, after)


def conv_back_body(
    ends, idx, grad_value, halo_value, value, halo_in, taps, gate_part, grad_step, w_value, w_step,
    low_value, tap_grads, c0, c1, c2, c3,
    grads, extended, low, product,
):
    row_count, width = grad_value.shape
    chunk = row_count // 4
    before, after = near_masks(ends, idx, row_count)
    grads[0:row_count, :] = grad_value[...]
    grads[row_count:, :] = halo_value[...]
    extended[0:8, :] = halo_in[...]
    extended[8:, :] = value[...]
    tap_grads[...] = jnp.zeros_like(tap_grads)
    for left in range(0, width, 128):
        span = slice(left, left + 128)
        rounded = taps_back(taps, grads, extended, row_count, span, before, after, tap_grads)
        low[:, span] = rounded
        low_value[:, span] = rounded.astype(F32)
    low_step = grad_step[:, 0 : w_step.shape[1]].astype(BF16)
    for left in range(0, D, 512):
        span = slice(left, left + 512)
        product[:, span] = (
            gate_part[:, span] + nt(low[...], w_value[span, :]) + nt(low_step, w_step[span, :])
        )
    for piece, target in enumerate((c0, c1, c2, c3)):
        place = pl.multiple_of((idx[1] ^ piece) * chunk, chunk)
        target[...] = product[pl.ds(place, chunk), :]


def conv_back(
    ends, idx, grad_value, halo_value, value, halo_in, gate_part, grad_step, params, weights, micro_count, row_count
):
    width = grad_value.shape[1]
    heads = weights.step.shape[1]
    total = micro_count * row_count
    chunk = row_count // 4
    return call(
        conv_back_body,
        (micro_count,),
        (ends, idx),
        [
            grad_value, halo_value, value, halo_in, params.taps, gate_part, grad_step, weights.value,
            weights.step,
        ],
        [
            rows(row_count, width),
            rows(8, width),
            rows(row_count, width),
            rows(8, width),
            whole((8, width)),
            rows(row_count, D),
            rows(row_count, 128),
            whole((D, width)),
            whole((D, heads)),
        ],
        [struct((total, width)), struct((micro_count * 8, width))] + [struct((micro_count * chunk, D))] * 4,
        [rows(row_count, width), rows(8, width)] + [rows(chunk, D)] * 4,
        [
            pltpu.VMEM((row_count + 8, width), F32),
            pltpu.VMEM((row_count + 8, width), F32),
            pltpu.VMEM((row_count, width), BF16),
            pltpu.VMEM((row_count, D), F32),
        ],
        flops=2 * total * width * D,
    )


def select_back_body(
    ends, idx, s0, s1, s2, s3, halo, select, halo_in, taps, grad_step,
    low_select, tap_grads, rest, grads, extended,
):
    row_count, columns = select.shape
    before, after = near_masks(ends, idx, row_count)
    grads[0:row_count, :] = (s0[...] + s1[...]) + (s2[...] + s3[...])
    grads[row_count:, :] = halo[...]
    extended[0:8, :] = halo_in[...]
    extended[8:, :] = select[...]
    tap_grads[...] = jnp.zeros_like(tap_grads)
    for left in range(0, columns, 128):
        span = slice(left, left + 128)
        rounded = taps_back(taps, grads, extended, row_count, span, before, after, tap_grads)
        low_select[:, span] = rounded.astype(F32)
    part = columns // 4
    rest[:, part:] = grad_step[:, 0 : 128 - part]
    for head in range(4):

        @pl.when(idx[1] == head)
        def _():
            rest[:, 0:part] = low_select[:, head * part : (head + 1) * part]


def select_back(ends, idx, selects, halo, select, halo_in, grad_step, params, micro_count, row_count):
    total, columns = select.shape
    right = halo_in.shape[1] // columns - 1
    return call(
        select_back_body,
        (micro_count,),
        (ends, idx),
        [*selects, halo, select, halo_in, params.taps, grad_step],
        [rows(row_count, columns)] * 4
        + [
            rows(8, columns),
            rows(row_count, columns),
            pl.BlockSpec((8, columns), lambda m, *_: (m, right)),
            pl.BlockSpec((8, columns), lambda m, *_: (0, right)),
            rows(row_count, 128),
        ],
        [struct((total, columns)), struct((micro_count * 8, columns)), struct((total, 128))],
        [rows(row_count, columns), rows(8, columns), rows(row_count, 128)],
        [pltpu.VMEM((row_count + 8, columns), F32), pltpu.VMEM((row_count + 8, columns), F32)],
        flops=30 * total * columns,
    )


def weight_body(idx, split, split_other, kept, kept_other, far, own, *, flip):
    def product(a, b):
        return tn(b, a) if flip else tn(a, b)

    low = kept[...].astype(BF16)
    low_other = kept_other[...].astype(BF16)
    result = product(split[...], low) + product(split_other[...].astype(BF16), low_other)

    @pl.when(pl.program_id(0) == 0)
    def _():
        far[...] = result

    @pl.when(pl.program_id(0) == 1)
    def _():
        own[...] = result


def weight_grad(idx, split, split_other, kept, kept_other, flip, marks=()):
    total, width = kept.shape
    block = split.shape[1] // 4
    shape = (width, block) if flip else (block, width)
    return call(
        partial(weight_body, flip=flip),
        (2,),
        (idx,),
        [split, split_other, kept, kept_other],
        [
            pl.BlockSpec((total, block), lambda b, idx: (0, idx[2] ^ (2 - 2 * b))),
            pl.BlockSpec((total, block), lambda b, idx: (0, b)),
            whole((total, width)),
            whole((total, width)),
        ],
        [struct(shape), struct(shape)],
        [whole(shape), whole(shape)],
        flops=8 * total * block * width,
        marks=marks,
    )


def join_body(idx, p0, p1, p2, p3, *refs):
    out = refs[-1]
    chunk = p0.shape[0]
    use_other = idx[3] == 1 if len(refs) > 1 else False

    def from_parts():
        for piece, part in enumerate((p0, p1, p2, p3)):
            out[pl.ds(pl.multiple_of((idx[1] ^ piece) * chunk, chunk), chunk), :] = part[...]

    if len(refs) == 1:
        from_parts()
    else:

        @pl.when(use_other)
        def _():
            out[...] = refs[0][...]

        pl.when(jnp.logical_not(use_other))(from_parts)


def join(idx, parts, other, micro_count, row_count):
    chunk = row_count // 4
    others = [] if other is None else [other]
    return call(
        join_body,
        (micro_count,),
        (idx,),
        [*parts, *others],
        [rows(chunk, D)] * 4 + [rows(row_count, D)] * len(others),
        [struct((micro_count * row_count, D))],
        [rows(row_count, D)],
    )[0]


def after(value, *others):
    return lax.optimization_barrier((value, *others))[0]


def shards(
    block_input,
    out_grad,
    lengths,
    norm_gain,
    gate_weight,
    value_weight,
    select_weight,
    step_weight,
    conv_value,
    conv_value_bias,
    conv_select,
    conv_select_bias,
    step_bias,
    log_rate,
    skip_gain,
    gate_gain,
    output_weight,
):
    micros, row_count, _ = block_input.shape
    total = micros * row_count
    width = gate_weight.shape[2]
    heads = width // P_SIZE
    chunk = row_count // 4
    tok_count = lax.axis_size(TOK)
    section, tok, head = (lax.axis_index(axis) for axis in AXES)
    ends = jnp.cumsum(lengths, axis=1).astype(jnp.int32)

    def scalars(flag, active):
        values = [tok * row_count, head, tok, flag, active]
        return jnp.stack([jnp.asarray(value, jnp.int32) for value in values])

    weights = SimpleNamespace(
        gain=norm_gain,
        gate=gate_weight[0],
        value=value_weight[0],
        select=select_weight[0],
        step=step_weight[0],
        out=output_weight[0],
        gate_gain=gate_gain[0].reshape(1, width),
    )
    taps = jnp.concatenate(
        [
            jnp.concatenate([conv_value[0].reshape(K, width), conv_select[0]], axis=1),
            jnp.concatenate([conv_value_bias[0].reshape(1, width), conv_select_bias], axis=1),
            jnp.zeros((3, width + 2 * NST), F32),
        ],
        axis=0,
    )
    params = SimpleNamespace(
        taps=taps,
        head_rows=jnp.pad(jnp.concatenate([step_bias, log_rate], axis=0), ((0, 6), (0, 128 - heads))),
        head_cols=jnp.pad(log_rate[0][:, None], ((0, 0), (0, 127))),
        skip=jnp.repeat(skip_gain[0], P_SIZE)[None, :],
    )

    def chunk_of(values):
        parts = values.reshape(micros, 4, chunk, values.shape[-1])
        mine = lax.dynamic_index_in_dim(parts, head, 1, keepdims=False)
        return mine.reshape(micros * chunk, values.shape[-1])

    def gather(values, layer):
        return [values] + [to_head(values, layer, step) for step in (1, 2, 3)]

    def reduce_chunks(parts, layer):
        moved = [to_head(parts[step], layer, step) for step in (1, 2, 3)]
        return (parts[0] + moved[0]) + (moved[1] + moved[2])

    def wave(layer, local, table, backward, ahead):
        decay = table.reshape(micros, row_count, 128)[:, row_count - 1, DECIN : DECIN + heads]
        shape = (micros, heads, P_SIZE, NST)
        entering, hops = (None, [])
        for hop in range(tok_count - 1):
            leaving = local
            if entering is not None:
                leaving = (
                    local.reshape(shape) + decay[:, :, None, None] * entering.reshape(shape)
                ).reshape(local.shape)
            source = tok_count - 1 - hop if backward else hop
            target = source - 1 if backward else source + 1

            def move(t, h, source=source, target=target):
                return (target if t == source else -1, h)

            if hop in ahead:
                leaving = after(leaving, *ahead[hop])
            hops.append(send(leaving, layer, move))
            entering = hops[-1] if entering is None else entering + hops[-1]
        return (entering, hops)

    def scan_forward(layer, parts, grads):
        idx = scalars(0, section == layer)
        normed, value, select, step = in_project(idx, parts, weights, micros, row_count)
        edge = jnp.concatenate(
            [
                value.reshape(micros, row_count, width)[:, row_count - 8 :],
                select.reshape(micros, row_count, 2 * NST)[:, row_count - 8 :],
            ],
            axis=-1,
        ).reshape(micros * 8, width + 2 * NST)
        halo = to_tok(edge, layer, 1)
        conv, table, table_t, state = conv_state(
            ends, idx, value, select, step, halo, params, micros, row_count
        )
        gate = gate_project(idx, after(normed, state), weights.gate)
        local = scan_local(ends, idx, conv, table, table_t, params, micros, row_count)
        entering, _ = wave(layer, state, table, False, {1: (gate, local)})
        scan, gated, sums = gate_mix(
            idx, local, conv, table, entering, gate, grads, micros, row_count
        )
        return SimpleNamespace(
            normed=normed, gate=gate, value=value, select=select, halo=halo, conv=conv, table=table,
            table_t=table_t, entering=entering, scan=scan, gated=gated, sums=gather(sums, layer),
        )

    def project_out(layer, saved, marks=()):
        idx = scalars(0, section == layer)
        scaled, *pieces = out_project(idx, saved.gated, saved.sums, weights, micros, row_count, marks)
        return (scaled, reduce_chunks(pieces, layer))

    def exchange(layer, values):
        return send(values, layer, lambda t, h: (t ^ 1, h))

    def split_blocks(values):
        block = values.shape[1] // 4
        return jnp.concatenate(
            [
                lax.dynamic_slice_in_dim(values, (tok ^ 3) * block, block, 1),
                lax.dynamic_slice_in_dim(values, (tok ^ 1) * block, block, 1),
            ],
            axis=1,
        ).astype(F32)

    def pair_product(layer, split, split_other, kept, other, flip=False, hold=(), marks=()):
        idx = scalars(0, section == layer)
        far, own = weight_grad(idx, split, split_other, kept, other, flip, marks)
        return (own, send(after(far, *hold), layer, lambda t, h: (t ^ 2, h)))

    def backward(layer, saved, grads, parts, plan):
        idx = scalars(0, section == layer)
        grad_gate, grad_scan, state, gain_grad, *given = gated_back(
            idx, grads, parts, saved.sums, saved.gate, saved.scan, saved.conv, saved.table, weights,
            micros, row_count,
        )
        state = after(state, *plan.before_wave)
        grad_x, grad_bc, grad_rows, skip_grad = scan_back(
            ends, idx, saved.conv, saved.table, saved.table_t, grad_scan, saved.entering, params,
            micros, row_count,
        )
        gate_part = lax.dot_general(
            after(grad_gate, grad_bc).astype(BF16),
            weights.gate,
            (((1,), (1,)), ((), ())),
            preferred_element_type=F32,
        )
        one, two = plan.in_wave(grad_gate, gate_part, given)
        later, hops = wave(
            layer, state, saved.table, True, {1: (grad_bc, *one), 2: (gate_part, *two)}
        )
        later = after(later, *plan.after_wave(grad_gate, hops))
        grad_value, grad_select, grad_step, small = scan_finish(
            idx, saved.conv, saved.table, saved.table_t, grad_x, grad_bc, grad_rows, later,
            saved.entering, params, micros, row_count,
        )
        first_value = grad_value.reshape(micros, row_count, width)[:, :8].reshape(micros * 8, width)
        halo_value = to_tok(first_value, layer, -1)
        selects = gather(grad_select, layer)
        first_select = grad_select.reshape(micros, row_count, 2 * NST)[:, :8].reshape(micros * 8, 2 * NST)
        halos = [
            send(first_select, layer, lambda t, h, step=step: (t - 1, h ^ step)) for step in range(4)
        ]
        waits = (*halos, *plan.before_conv(grad_step, (halo_value, *halos)))
        low_value, value_taps, *pieces = conv_back(
            ends, idx, after(grad_value, *waits), halo_value, saved.value, saved.halo, gate_part, grad_step,
            params, weights, micros, row_count,
        )
        grad_sum = reduce_chunks(pieces, layer)
        selects = [selects[0]] + [after(part, grad_sum) for part in selects[1:]]
        halo_select = sum(halos)
        grad_normed = after(grad_sum, *plan.beside_sum(pieces[0], low_value))
        low_select, select_taps, rest = select_back(
            ends, idx, selects, halo_select, saved.select, saved.halo, grad_step, params, micros, row_count
        )
        grad_normed = grad_normed + lax.dot_general(
            chunk_of(low_select).astype(BF16),
            weights.select,
            (((1,), (1,)), ((), ())),
            preferred_element_type=F32,
        )
        hidden = saved.chunk_in
        inv = lax.rsqrt(jnp.mean(hidden * hidden, axis=-1, keepdims=True) + EPSILON)
        norm_grad = jnp.sum(grad_normed * hidden * inv, axis=0)
        weighted = grad_normed * weights.gain
        grad_hidden = (
            saved.grad_chunk
            + inv * weighted
            - hidden * (inv * inv * inv) * jnp.mean(weighted * hidden, axis=-1, keepdims=True)
        )
        sums = (
            norm_grad,
            jnp.concatenate(
                [
                    value_taps.reshape(micros, 8, -1)[:, : K + 1].sum(0).reshape(-1),
                    select_taps.reshape(micros, 8, -1)[:, : K + 1].sum(0).reshape(-1),
                    gain_grad.reshape(micros, 8, -1)[:, 0].sum(0),
                    small.reshape(micros, heads, 128).sum(0)[:, :2].T.reshape(-1),
                    skip_grad.reshape(micros, heads, 128).sum(0)[:, 0],
                ]
            ),
        )
        return (grad_hidden, SimpleNamespace(gate=grad_gate, value=low_value, rest=rest), sums)

    first = section == 0
    pairwise = tok_count == 4
    grad_rows_1 = out_grad.reshape(total, D)
    scaled_grads_1 = back_project(scalars(0, section == 1), grad_rows_1, weights.out, micros, row_count)

    input_rows = block_input.reshape(total, D)
    saved_0 = scan_forward(0, [input_rows], [])
    saved_0.chunk_in = chunk_of(input_rows).astype(F32)
    saved_0.scaled, saved_0.branch = project_out(0, saved_0)
    out_0 = moved = saved_0.chunk_in + saved_0.branch
    if pairwise:
        grad_other_1 = exchange(1, split_blocks(grad_rows_1))
        moved = after(out_0, grad_other_1, scaled_grads_1)

    chunk_1 = lax.ppermute(moved, SECTION, [(0, 1)])
    parts_1 = gather(chunk_1, 1)
    if pairwise:
        other_0 = exchange(0, after(split_blocks(saved_0.normed), out_0))
        scaled_0 = exchange(0, after(saved_0.scaled, out_0))
        parts_1[0] = after(parts_1[0], other_0, scaled_0)
    saved_1 = scan_forward(1, parts_1, [scaled_grads_1, weights.gate_gain])
    saved_1.chunk_in = chunk_1
    saved_1.grad_chunk = chunk_of(grad_rows_1).astype(F32)

    work = SimpleNamespace()
    before_wave_1 = ()
    if pairwise:
        other_1 = exchange(1, after(split_blocks(saved_1.normed), saved_1.entering))
        before_wave_1 = (other_1,)

    def in_wave_1(grad_gate, gate_part, given):
        saved_1.scaled = given[0]
        work.kept_gate = grad_gate
        return ((), ())

    def after_wave_1(grad_gate, hops):
        if pairwise:
            work.gate_other = exchange(1, after(grad_gate, hops[0]))
        return ()

    def before_conv_1(done, halo):
        if not pairwise:
            return ()
        work.gate_1 = pair_product(
            1, saved_1.normed, other_1, after(work.kept_gate, done), work.gate_other, hold=halo
        )
        return (work.gate_1[0],)

    def beside_sum_1(piece, low_value):
        if pairwise:
            work.value_other = exchange(1, low_value)
            return (work.gate_1[1], work.value_other)
        return ()

    grad_mid, kept_1, sums_1 = backward(
        1, saved_1, scaled_grads_1, None,
        SimpleNamespace(
            before_wave=before_wave_1, in_wave=in_wave_1, after_wave=after_wave_1, before_conv=before_conv_1,
            beside_sum=beside_sum_1,
        ),
    )

    saved_0.grad_chunk = lax.ppermute(grad_mid, SECTION, [(1, 0)])
    low_chunk = lax.reduce_precision(saved_0.grad_chunk, 8, 7)
    inner = jnp.sum(low_chunk * saved_0.branch, axis=-1, keepdims=True) / (H * P_SIZE)
    payload = jnp.concatenate(
        [saved_0.grad_chunk, jnp.broadcast_to(inner, (micros * chunk, PAD))], axis=1
    )
    parts_0 = gather(payload, 0)
    before_wave_0 = ()
    if pairwise:
        work.value_1 = pair_product(
            1, saved_1.normed, other_1, kept_1.value, after(work.value_other, grad_mid)
        )
        parts_0[0] = after(parts_0[0], work.value_1[0])

    def tell(values):
        return lax.ppermute(values[:8, :128], SECTION, [(0, 1)])

    def in_wave_0(grad_gate, gate_part, given):
        work.low_grad_0, work.full_0 = given
        work.kept_gate_0 = grad_gate
        marks = (work.value_1[1][:8, :128],) if pairwise else ()
        _, branch = project_out(1, saved_1, marks)
        work.out_1 = chunk_1 + branch
        work.shown_1 = gather(work.out_1, 1)
        return ((), ())

    def after_wave_0(grad_gate, hops):
        if not pairwise:
            return (work.out_1,)
        work.gate_other_0 = exchange(0, after(grad_gate, hops[0]))
        work.grad_other_0 = exchange(0, after(split_blocks(work.low_grad_0), hops[-1]))
        return (work.out_1,)

    def before_conv_0(done, halo):
        if not pairwise:
            return ()
        work.gate_0 = pair_product(
            0, saved_0.normed, other_0, after(work.kept_gate_0, done), work.gate_other_0, hold=halo
        )
        return (work.gate_0[0], *work.shown_1)

    def beside_sum_0(piece, low_value):
        if not pairwise:
            return ()
        work.value_other_0 = exchange(0, low_value)
        work.scaled_0 = pair_product(
            0, work.low_grad_0, work.grad_other_0, after(saved_0.scaled, piece), scaled_0, True
        )
        mark = tell(piece)
        scaled_other = exchange(1, after(saved_1.scaled, mark))
        work.scaled_1 = pair_product(
            1, grad_rows_1, grad_other_1, saved_1.scaled, scaled_other, True, marks=(mark,)
        )
        return (work.scaled_0[0],)

    grad_in, kept_0, sums_0 = backward(
        0, saved_0, None, parts_0,
        SimpleNamespace(
            before_wave=before_wave_0, in_wave=in_wave_0, after_wave=after_wave_0, before_conv=before_conv_0,
            beside_sum=beside_sum_0,
        ),
    )
    shown_0 = gather(grad_in, 0)

    def chosen(left, right):
        return jnp.where(first, left, right)

    rest_sum = chosen(
        tn(saved_0.normed, kept_0.rest.astype(BF16)), tn(saved_1.normed, kept_1.rest.astype(BF16))
    )
    norm_sum, head_sum = (chosen(left, right) for left, right in zip(sums_0, sums_1, strict=True))
    packed = jnp.concatenate([norm_sum, head_sum])
    size = -(-packed.size // 1024) * 1024
    packed = jnp.pad(packed, (0, size - packed.size)).reshape(-1, 128)
    block = D // tok_count

    def block_of(which):
        return lax.dynamic_slice_in_dim(rest_sum, which * block, block, 0)

    if pairwise:
        total_sum = jnp.concatenate([block_of(tok), packed], axis=0)
        for step in (1, 2, 3):
            total_sum = total_sum + lax.ppermute(
                jnp.concatenate([block_of(tok ^ step), packed], axis=0),
                TOK,
                [(source, source ^ step) for source in range(4)],
            )
        rest_sum, packed = (total_sum[:block], total_sum[block:])
    else:
        rest_sum = lax.psum_scatter(rest_sum, TOK, scatter_dimension=0, tiled=True)
        packed = lax.psum(packed, TOK)
    quarter = 2 * NST // 4
    packed = packed.reshape(-1)
    norm_sum, head_sum = (lax.dynamic_slice_in_dim(packed[:D], tok * block, block, 0), packed[D:])
    lanes = jnp.concatenate(
        [rest_sum[:, :quarter], jnp.broadcast_to(norm_sum[:, None], (block, 128 - quarter))], axis=1
    )
    norm_sum = norm_sum[:, None]
    select_sum = jnp.zeros((block, 2 * NST), F32)
    for step in range(4):
        moved = lanes
        if step > 0:
            moved = lax.ppermute(lanes, HEAD, [(source, source ^ step) for source in range(4)])
            norm_sum = norm_sum + moved[:, quarter : quarter + 1]
        select_sum = lax.dynamic_update_slice_in_dim(
            select_sum, moved[:, :quarter], (head ^ step) * quarter, 1
        )
    norm_sum = norm_sum[:, 0]

    if pairwise:
        work.value_0 = pair_product(
            0, saved_0.normed, other_0, after(kept_0.value, grad_in, work.scaled_0[1]), work.value_other_0
        )
        parts_1[0] = after(parts_1[0], work.value_0[0])
        work.full_0 = after(work.full_0, work.value_0[0])
    full_1 = join(scalars(0, section == 1), parts_1, None, micros, row_count)
    layer_out = join(
        scalars(first, 1), work.shown_1, lax.ppermute(full_1, SECTION, [(1, 0)]), micros, row_count
    )
    full_0 = lax.ppermute(work.full_0, SECTION, [(0, 1)])
    input_grad = join(scalars(section == 1, 1), shown_0, full_0, micros, row_count)
    if pairwise:
        scaled_sum, gate_sum, value_sum = (
            chosen(left[0] + after(left[1], *waits), right[0] + right[1])
            for left, right, waits in (
                (work.scaled_0, work.scaled_1, ()),
                (work.gate_0, work.gate_1, ()),
                (work.value_0, work.value_1, (select_sum, layer_out, input_grad)),
            )
        )
    else:
        normed = chosen(saved_0.normed, saved_1.normed)

        def scattered(left, right, axis):
            return lax.psum_scatter(
                tn(left.astype(BF16), right.astype(BF16)), TOK, scatter_dimension=axis, tiled=True
            )

        scaled_sum = scattered(
            chosen(saved_0.scaled, saved_1.scaled), chosen(work.low_grad_0, grad_rows_1), 1
        )
        gate_sum, value_sum = (
            scattered(normed, chosen(left, right), 0)
            for left, right in ((kept_0.gate, kept_1.gate), (kept_0.value, kept_1.value))
        )
    pieces, place = ([], 0)
    for shape in ((K + 1, width), (K + 1, 2 * NST), (heads, P_SIZE), (heads,), (heads,), (heads,)):
        size = 1
        for extent in shape:
            size *= extent
        pieces.append(head_sum[place : place + size].reshape(shape))
        place += size
    value_taps, select_taps, gain_sum, bias_sum, rate_sum, skip_sum = pieces

    def mine(values, axis):
        size = values.shape[axis] // tok_count
        return lax.dynamic_slice_in_dim(values, tok * size, size, axis)

    outs = (
        layer_out.reshape(micros, row_count, D),
        input_grad.reshape(micros, row_count, D),
        norm_sum,
        gate_sum,
        value_sum,
        select_sum,
        rest_sum[:, quarter : quarter + heads],
        mine(value_taps[:K].reshape(K, heads, P_SIZE), 2),
        mine(value_taps[K].reshape(heads, P_SIZE), 1),
        mine(select_taps[:K], 1),
        mine(select_taps[K], 0),
        bias_sum,
        rate_sum,
        skip_sum,
        mine(gain_sum, 1),
        scaled_sum,
    )
    return tuple(value[None] for value in outs)


def solution(mesh):
    return jax.shard_map(
        shards,
        mesh=mesh,
        in_specs=(
            P(None, TOK, None),
            P(None, TOK, None),
            P(),
            P(SECTION, None),
            P(SECTION, None, HEAD),
            P(SECTION, None, HEAD),
            P(SECTION, None, None),
            P(SECTION, None, HEAD),
            P(SECTION, None, HEAD, None),
            P(SECTION, HEAD, None),
            P(SECTION, None, None),
            P(SECTION, None),
            P(SECTION, HEAD),
            P(SECTION, HEAD),
            P(SECTION, HEAD),
            P(SECTION, HEAD, None),
            P(SECTION, HEAD, None),
        ),
        out_specs=(
            P(SECTION, None, TOK, None),
            P(SECTION, None, TOK, None),
            P(SECTION, TOK),
            P(SECTION, TOK, HEAD),
            P(SECTION, TOK, HEAD),
            P(SECTION, TOK, None),
            P(SECTION, TOK, HEAD),
            P(SECTION, None, HEAD, TOK),
            P(SECTION, HEAD, TOK),
            P(SECTION, None, TOK),
            P(SECTION, TOK),
            P(SECTION, HEAD),
            P(SECTION, HEAD),
            P(SECTION, HEAD),
            P(SECTION, HEAD, TOK),
            P(SECTION, HEAD, TOK),
        ),
        check_vma=False,
    )
```

```python
from functools import partial
from types import SimpleNamespace

import jax
import jax.numpy as jnp
from jax import lax
from jax.experimental import pallas as pl
from jax.experimental.pallas import tpu as pltpu
from jax.sharding import PartitionSpec as P

D = 2048
H = 64
P_SIZE = 64
NST = 128
K = 4
EPSILON = 1e-05
SECTION, TOK, HEAD = AXES = ("section", "tok", "head")
F32 = jnp.float32
BF16 = jnp.bfloat16
EXACT = lax.Precision.HIGHEST
VMEM_BYTES = 58 * 1024 * 1024
PAD = 128

DT, CUM, SIG, LOG, ENDW, DECIN, BASE = (0, 16, 32, 48, 64, 80, 96)


def send(value, section, move):
    tok_count, head_count = (lax.axis_size(TOK), lax.axis_size(HEAD))

    def flat(tok, head):
        return (section * tok_count + tok) * head_count + head

    pairs = []
    for tok in range(tok_count):
        for head in range(head_count):
            target = move(tok, head)
            if 0 <= target[0] < tok_count:
                pairs.append((flat(tok, head), flat(*target)))
    return lax.ppermute(value, AXES, pairs)


def to_head(value, section, step):
    return send(value, section, lambda tok, head: (tok, head ^ step))


def to_tok(value, section, step):
    return send(value, section, lambda tok, head: (tok + step, head))


def nn(left, right, precision=None):
    return lax.dot_general(
        left, right, (((1,), (0,)), ((), ())), precision=precision, preferred_element_type=F32
    )


def nt(left, right, precision=None):
    return lax.dot_general(
        left, right, (((1,), (1,)), ((), ())), precision=precision, preferred_element_type=F32
    )


def tn(left, right):
    return lax.dot_general(left, right, (((0,), (0,)), ((), ())), preferred_element_type=F32)


def split(values):
    high = values.astype(BF16)
    return (high, (values - high.astype(F32)).astype(BF16))


def fine(product, left, right):
    return product(left[0], right[0]) + (product(left[0], right[1]) + product(left[1], right[0]))


def act_of(values):
    return values * sigmoid(values)


def sigmoid(values):
    return 1.0 / (1.0 + jnp.exp(-values))


def seg_at(points, ends, micro):
    inside = (points >= ends[micro, 0]).astype(jnp.int32)
    for which in range(1, 4):
        inside = inside + (points >= ends[micro, which]).astype(jnp.int32)
    return jnp.where(points >= 0, inside, -1)


def call(body, grid, scalars, ins, in_specs, outs, out_specs, scratch=(), flops=0, marks=()):
    flag = len(scalars) - 1
    read = len(scalars) + len(ins)

    def guarded(*refs):
        @pl.when(refs[flag][4] == 1)
        def _():
            body(*refs[:read], *refs[read + len(marks) :])

    moved = sum(a.size * a.dtype.itemsize for a in ins)
    moved += sum(o.size * o.dtype.itemsize for o in outs)
    return pl.pallas_call(
        guarded,
        grid_spec=pltpu.PrefetchScalarGridSpec(
            num_scalar_prefetch=len(scalars),
            grid=grid,
            in_specs=in_specs + [whole(mark.shape) for mark in marks],
            out_specs=out_specs,
            scratch_shapes=list(scratch),
        ),
        out_shape=outs,
        compiler_params=pltpu.CompilerParams(vmem_limit_bytes=VMEM_BYTES),
        cost_estimate=pl.CostEstimate(flops=flops, bytes_accessed=moved, transcendentals=0),
    )(*scalars, *ins, *marks)


def rows(count, width):
    return pl.BlockSpec((count, width), lambda m, *_: (m, 0))


def whole(shape):
    return pl.BlockSpec(shape, lambda m, *_: (0,) * len(shape))


def struct(shape, dtype=F32):
    return jax.ShapeDtypeStruct(shape, dtype)


def pair_of(table, base, pair, lane):
    first = table[:, base + 2 * pair : base + 2 * pair + 1]
    second = table[:, base + 2 * pair + 1 : base + 2 * pair + 2]
    return jnp.where(lane < P_SIZE, first, second)


def head_sums(values, pair, head_count):
    owner = lax.broadcasted_iota(jnp.int32, (head_count, 2 * P_SIZE), 0)
    lane = lax.broadcasted_iota(jnp.int32, (head_count, 2 * P_SIZE), 1)
    chosen = (owner == 2 * pair + (lane >= P_SIZE).astype(jnp.int32)).astype(BF16)
    high = values.astype(BF16)
    low = (values - high.astype(F32)).astype(BF16)
    return nt(chosen, high) + nt(chosen, low)


def in_body(idx, *refs, part_count, micro_count, row_count):
    parts, refs = (refs[:part_count], refs[part_count:])
    gain, w_value, w_select, w_step, normed, value, select, step = refs
    chunk = row_count // 4
    step_id = pl.program_id(0)

    @pl.when(step_id == 0)
    def _():
        for micro in range(micro_count):
            for piece in range(4):
                if part_count == 1:
                    place = micro * row_count + piece * chunk
                    values = parts[0][place : place + chunk, :].astype(F32)
                else:
                    place = pl.multiple_of(micro * row_count + (idx[1] ^ piece) * chunk, chunk)
                    values = parts[piece][micro * chunk : (micro + 1) * chunk, :]
                inv = lax.rsqrt(jnp.mean(values * values, axis=-1, keepdims=True) + EPSILON)
                normed[pl.ds(place, chunk), :] = (values * inv * gain[...]).astype(BF16)
        select[...] = nn(normed[...], w_select[...])
        step[...] = nn(normed[...], w_step[...])

    value[...] = nn(normed[...], w_value[...])


def in_project(idx, parts, weights, micro_count, row_count):
    total = micro_count * row_count
    width = weights.value.shape[1]
    heads = weights.step.shape[1]
    tile = width // 4
    outs = [
        struct((total, D), BF16),
        struct((total, width)),
        struct((total, 2 * NST)),
        struct((total, heads)),
    ]
    cols = pl.BlockSpec((total, tile), lambda j, *_: (0, j))
    wcols = pl.BlockSpec((D, tile), lambda j, *_: (0, j))
    return call(
        partial(in_body, part_count=len(parts), micro_count=micro_count, row_count=row_count),
        (4,),
        (idx,),
        [*parts, weights.gain, weights.value, weights.select, weights.step],
        [whole(part.shape) for part in parts]
        + [whole((1, D)), wcols, whole((D, 2 * NST)), whole((D, heads))],
        outs,
        [whole((total, D)), cols, whole((total, 2 * NST)), whole((total, heads))],
        flops=2 * total * D * (width + 2 * NST),
    )


def gate_body(idx, normed, w_gate, gate):
    gate[...] = nn(normed[...], w_gate[...])


def gate_project(idx, normed, w_gate):
    total, width = (normed.shape[0], w_gate.shape[1])
    tile = width // 4
    return call(
        gate_body,
        (4,),
        (idx,),
        [normed, w_gate],
        [whole((total, D)), pl.BlockSpec((D, tile), lambda j, *_: (0, j))],
        [struct((total, width))],
        [pl.BlockSpec((total, tile), lambda j, *_: (0, j))],
        flops=2 * total * D * width,
    )[0]


def conv_body(
    ends, idx, value, select, step, halo, taps, head_rows,
    conv, table, table_t, state, extended, weighted, weighted_low,
):
    micro = pl.program_id(0)
    row_count, width = value.shape
    heads = step.shape[1]
    base = idx[0]
    at = base + lax.broadcasted_iota(jnp.int32, (row_count, 1), 0)
    seg = seg_at(at, ends, micro)
    seg_before = seg_at(base - 1 + jnp.zeros((1, 1), jnp.int32), ends, micro)
    seg_last = seg_at(base + row_count - 1 + jnp.zeros((1, 1), jnp.int32), ends, micro)
    carry = (seg == seg_before).astype(F32)
    tail = (seg == seg_last).astype(F32)

    pre = step[...] + head_rows[0:1, 0:heads]
    step_size = jnp.maximum(pre, 0.0) + jnp.log1p(jnp.exp(-jnp.abs(pre)))
    log_decay = -jnp.exp(head_rows[1:2, 0:heads]) * step_size
    row_id = lax.broadcasted_iota(jnp.int32, (row_count, row_count), 0)
    col_id = lax.broadcasted_iota(jnp.int32, (row_count, row_count), 1)
    cum = nn((row_id >= col_id).astype(F32), log_decay, EXACT)
    end_base = jnp.exp(cum[row_count - 1 : row_count, :] - cum) * tail
    decay_in = jnp.exp(cum) * carry
    table[...] = jnp.zeros_like(table)
    for place, part in (
        (DT, step_size),
        (CUM, cum),
        (SIG, sigmoid(pre)),
        (LOG, log_decay),
        (ENDW, end_base * step_size),
        (DECIN, decay_in),
        (BASE, end_base),
    ):
        table[:, place : place + heads] = part
    table_t[...] = table[...].T

    extended[0:8, :] = halo[...]
    extended[8:, 0:width] = value[...]
    extended[8:, width:] = select[...]
    masks = [(seg_at(at - (K - 1 - tap), ends, micro) == seg).astype(F32) for tap in range(K - 1)]
    lane = lax.broadcasted_iota(jnp.int32, (row_count, 128), 1)
    columns = width + 2 * NST
    for left in range(0, columns, 128):
        span = slice(left, left + 128)
        total = taps[4:5, span] + taps[3:4, span] * extended[8 : 8 + row_count, span]
        for tap in range(K - 1):
            total = total + taps[tap : tap + 1, span] * (
                extended[5 + tap : 5 + tap + row_count, span] * masks[tap]
            )
        conv[:, span] = total
        if left < width:
            weighted[:, span], weighted_low[:, span] = split(
                act_of(total) * pair_of(table[...], ENDW, left // 128, lane)
            )
    b_act = split(act_of(conv[:, width : width + NST]))
    state[...] = fine(tn, (weighted[...], weighted_low[...]), b_act)


def conv_state(ends, idx, value, select, step, halo, params, micro_count, row_count):
    width = value.shape[1]
    heads = step.shape[1]
    total = micro_count * row_count
    return call(
        conv_body,
        (micro_count,),
        (ends, idx),
        [value, select, step, halo, params.taps, params.head_rows],
        [
            rows(row_count, width),
            rows(row_count, 2 * NST),
            rows(row_count, heads),
            rows(8, width + 2 * NST),
            whole((8, width + 2 * NST)),
            whole((8, 128)),
        ],
        [
            struct((total, width + 2 * NST)),
            struct((total, 128)),
            struct((micro_count * 128, row_count)),
            struct((micro_count * width, NST)),
        ],
        [
            rows(row_count, width + 2 * NST),
            rows(row_count, 128),
            rows(128, row_count),
            rows(width, NST),
        ],
        [
            pltpu.VMEM((row_count + 8, width + 2 * NST), F32),
            pltpu.VMEM((row_count, width), BF16),
            pltpu.VMEM((row_count, width), BF16),
        ],
        flops=40 * total * width,
    )


def mask_bias(ends, idx, micro, row_count):
    base = idx[0]
    seg_col = seg_at(base + lax.broadcasted_iota(jnp.int32, (row_count, 1), 0), ends, micro)
    seg_row = seg_at(base + lax.broadcasted_iota(jnp.int32, (1, row_count), 1), ends, micro)
    row_id = lax.broadcasted_iota(jnp.int32, (row_count, row_count), 0)
    col_id = lax.broadcasted_iota(jnp.int32, (row_count, row_count), 1)
    return jnp.where((seg_col == seg_row) & (row_id >= col_id), 0.0, -1e30)


def sides(values, lane):
    return (
        split(jnp.where(lane < P_SIZE, values, 0.0)),
        split(jnp.where(lane < P_SIZE, 0.0, values)),
    )


def scan_body(ends, idx, conv, table, table_t, skip, out, scores, bias):
    micro = pl.program_id(0)
    row_count = conv.shape[0]
    width = conv.shape[1] - 2 * NST
    half = row_count // 2
    b_act = split(act_of(conv[:, width : width + NST]))
    c_act = split(act_of(conv[:, width + NST :]))
    scores[...] = fine(nt, c_act, b_act)
    bias[...] = mask_bias(ends, idx, micro, row_count)
    lane = lax.broadcasted_iota(jnp.int32, (row_count, 128), 1)
    for pair in range(width // 128):
        span = slice(128 * pair, 128 * pair + 128)
        x_act = act_of(conv[:, span])
        halves = sides(x_act * pair_of(table[...], DT, pair, lane), lane)
        direct = skip[:, span] * x_act
        for top, bottom in ((0, half), (half, row_count)):
            result = direct[top:bottom, :]
            for side in range(2):
                head = 2 * pair + side
                cum_col = table[top:bottom, CUM + head : CUM + head + 1]
                cum_row = table_t[CUM + head : CUM + head + 1, 0:bottom]
                decay = jnp.exp(cum_col - cum_row + bias[top:bottom, 0:bottom])
                mixing = split(decay * scores[top:bottom, 0:bottom])
                result = result + fine(nn, mixing, [part[0:bottom, :] for part in halves[side]])
            out[top:bottom, span] = result


def scan_local(ends, idx, conv, table, table_t, params, micro_count, row_count):
    width = conv.shape[1] - 2 * NST
    return call(
        scan_body,
        (micro_count,),
        (ends, idx),
        [conv, table, table_t, params.skip],
        [rows(row_count, width + 2 * NST), rows(row_count, 128), rows(128, row_count), whole((1, width))],
        [struct((micro_count * row_count, width))],
        [rows(row_count, width)],
        [pltpu.VMEM((row_count, row_count), F32), pltpu.VMEM((row_count, row_count), F32)],
        flops=30 * micro_count * row_count * row_count * (width // P_SIZE),
    )[0]


def mix_body(idx, local, select, table, entering, gate, *refs):
    grads, (scan, gated, sums) = (refs[:-3], refs[-3:])
    row_count, width = local.shape
    c_act = split(act_of(select[:, NST:]))
    lane = lax.broadcasted_iota(jnp.int32, (row_count, 128), 1)
    squares = jnp.zeros((row_count, 128), F32)
    inner = jnp.zeros((row_count, 128), F32)
    for pair in range(width // 128):
        span = slice(128 * pair, 128 * pair + 128)
        carried = fine(nt, c_act, split(entering[span, :]))
        value = local[:, span] + carried * pair_of(table[...], DECIN, pair, lane)
        scan[:, span] = value
        result = value * act_of(gate[:, span])
        gated[:, span] = result
        squares = squares + result * result
        if grads:
            inner = inner + result * (grads[0][:, span] * grads[1][:, span])
    ones = jnp.ones((4, 128), F32)
    sums[0:4, :] = nt(ones, squares, EXACT)
    sums[4:8, :] = nt(ones, inner, EXACT)


def gate_mix(idx, local, conv, table, entering, gate, grads, micro_count, row_count):
    width = local.shape[1]
    total = micro_count * row_count
    select_block = pl.BlockSpec((row_count, 2 * NST), lambda m, *_: (m, width // (2 * NST)))
    return call(
        mix_body,
        (micro_count,),
        (idx,),
        [local, conv, table, entering, gate, *grads],
        [
            rows(row_count, width),
            select_block,
            rows(row_count, 128),
            rows(width, NST),
            rows(row_count, width),
        ]
        + ([rows(row_count, width), whole((1, width))] if grads else []),
        [struct((total, width)), struct((total, width)), struct((micro_count * 8, row_count))],
        [rows(row_count, width), rows(row_count, width), rows(8, row_count)],
        flops=6 * total * width * NST,
    )


def back_body(idx, grad, w_out, out):
    out[...] = nt(grad[...], w_out[...])


def back_project(idx, grad, w_out, micro_count, row_count):
    total, width = (grad.shape[0], w_out.shape[0])
    tile = width // 4
    return call(
        back_body,
        (4,),
        (idx,),
        [grad, w_out],
        [whole((total, D)), pl.BlockSpec((tile, D), lambda j, *_: (j, 0))],
        [struct((total, width))],
        [pl.BlockSpec((total, tile), lambda j, *_: (0, j))],
        flops=2 * total * width * D,
    )[0]


def norms_of(sums):
    total = ((sums[0][...] + sums[1][...]) + (sums[2][...] + sums[3][...])) / (H * P_SIZE)
    total = total.T
    inv = lax.rsqrt(total[:, 0:1] + EPSILON)
    return (inv, total[:, 4:5] * inv)


def out_body(idx, gated, s0, s1, s2, s3, gain, w_out, scaled, *refs):
    chunks, (low, product) = (refs[:4], refs[4:])
    row_count, width = gated.shape
    chunk = row_count // 4
    inv, _ = norms_of((s0, s1, s2, s3))
    for left in range(0, width, 128):
        span = slice(left, left + 128)
        rounded = (gated[:, span] * inv * gain[:, span]).astype(BF16)
        low[:, span] = rounded
        scaled[:, span] = rounded.astype(F32)
    for left in range(0, D, 512):
        product[:, left : left + 512] = nn(low[...], w_out[:, left : left + 512])
    for piece in range(4):
        place = pl.multiple_of((idx[1] ^ piece) * chunk, chunk)
        chunks[piece][...] = product[pl.ds(place, chunk), :]


def out_project(idx, gated, sums, weights, micro_count, row_count, marks=()):
    width = gated.shape[1]
    total = micro_count * row_count
    chunk = row_count // 4
    return call(
        out_body,
        (micro_count,),
        (idx,),
        [gated, *sums, weights.gate_gain, weights.out],
        [rows(row_count, width)] + [rows(8, row_count)] * 4 + [whole((1, width)), whole((width, D))],
        [struct((total, width))] + [struct((micro_count * chunk, D))] * 4,
        [rows(row_count, width)] + [rows(chunk, D)] * 4,
        [pltpu.VMEM((row_count, width), BF16), pltpu.VMEM((row_count, D), F32)],
        flops=2 * total * width * D,
        marks=marks,
    )


def gated_body(idx, *refs, from_parts):
    sums, (gate, scan, select, table, gain), refs = (refs[:4], refs[4:9], refs[9:])
    if from_parts:
        parts, w_out, refs = (refs[:4], refs[4], refs[5:])
    else:
        grads, refs = (refs[0], refs[1:])
    grad_gate, grad_scan, state, gain_grad = refs[:4]
    if from_parts:
        low_grad, full, norms = refs[4:7]
    else:
        scaled = refs[4]
    carried, carried_low = refs[-2:]
    row_count, width = gate.shape
    chunk = row_count // 4
    inv, inner = norms_of(sums)
    if from_parts:
        for piece in range(4):
            place = pl.ds(pl.multiple_of((idx[1] ^ piece) * chunk, chunk), chunk)
            values = parts[piece][:, 0:D]
            full[place, :] = values
            low_grad[place, :] = values.astype(BF16)
            norms[place, :] = parts[piece][:, D:]
        inner = norms[:, 0:1]
    c_act = split(act_of(select[:, NST:]))
    lane = lax.broadcasted_iota(jnp.int32, (row_count, 128), 1)
    gain_grad[...] = jnp.zeros_like(gain_grad)
    for pair in range(width // 128):
        span = slice(128 * pair, 128 * pair + 128)
        grad_scaled = nt(low_grad[...], w_out[span, :]) if from_parts else grads[:, span]
        gate_pre = gate[:, span]
        sig = sigmoid(gate_pre)
        act = gate_pre * sig
        out = scan[:, span]
        normal = out * act * inv
        gain_grad[0:1, span] = jnp.sum(grad_scaled * normal, axis=0, keepdims=True)
        if not from_parts:
            scaled[:, span] = (normal * gain[:, span]).astype(BF16).astype(F32)
        grad_gated = inv * (grad_scaled * gain[:, span]) - normal * (inv * inner)
        grad_out = grad_gated * act
        grad_scan[:, span] = grad_out
        grad_gate[:, span] = (
            (grad_gated * out * (sig * (1.0 + gate_pre * (1.0 - sig)))).astype(BF16).astype(F32)
        )
        carried[:, span], carried_low[:, span] = split(
            grad_out * pair_of(table[...], DECIN, pair, lane)
        )
    state[...] = fine(tn, (carried[...], carried_low[...]), c_act)


def gated_back(idx, grads, parts, sums, gate, scan, conv, table, weights, micro_count, row_count):
    width = gate.shape[1]
    total = micro_count * row_count
    chunk = row_count // 4
    from_parts = grads is None
    select_block = pl.BlockSpec((row_count, 2 * NST), lambda m, *_: (m, width // (2 * NST)))
    ins = [*sums, gate, scan, conv, table, weights.gate_gain]
    in_specs = [rows(8, row_count)] * 4 + [
        rows(row_count, width),
        rows(row_count, width),
        select_block,
        rows(row_count, 128),
        whole((1, width)),
    ]
    outs = [
        struct((total, width)),
        struct((total, width)),
        struct((micro_count * width, NST)),
        struct((micro_count * 8, width)),
    ]
    out_specs = [rows(row_count, width), rows(row_count, width), rows(width, NST), rows(8, width)]
    scratch = [pltpu.VMEM((row_count, width), BF16), pltpu.VMEM((row_count, width), BF16)]
    if from_parts:
        ins += [*parts, weights.out]
        in_specs += [rows(chunk, D + PAD)] * 4 + [whole((width, D))]
        outs += [struct((total, D), BF16), struct((total, D))]
        out_specs += [rows(row_count, D), rows(row_count, D)]
        scratch = [pltpu.VMEM((row_count, PAD), F32)] + scratch
    else:
        ins.append(grads)
        in_specs.append(rows(row_count, width))
        outs.append(struct((total, width)))
        out_specs.append(rows(row_count, width))
    return call(
        partial(gated_body, from_parts=from_parts),
        (micro_count,),
        (idx,),
        ins,
        in_specs,
        outs,
        out_specs,
        scratch,
        flops=2 * total * width * (D if from_parts else NST),
    )


def scan_back_body(
    ends, idx, conv, table, table_t, grad, entering, skip,
    grad_x, grad_bc, grad_rows, skip_grad,
    scores, bias, grad_scores, row_sums, col_sums,
):
    micro = pl.program_id(0)
    row_count, width = grad.shape
    heads = width // P_SIZE
    half = row_count // 2
    b_act = split(act_of(conv[:, width : width + NST]))
    c_act = split(act_of(conv[:, width + NST :]))
    scores[...] = fine(nt, c_act, b_act)
    bias[...] = mask_bias(ends, idx, micro, row_count)
    grad_scores[...] = jnp.zeros_like(grad_scores)
    row_sums[...] = jnp.zeros_like(row_sums)
    lane = lax.broadcasted_iota(jnp.int32, (row_count, 128), 1)
    grad_c = jnp.zeros((row_count, NST), F32)
    cum_grad = jnp.zeros((heads, row_count), F32)
    step_grad = jnp.zeros((heads, row_count), F32)
    direct_sum = jnp.zeros((heads, row_count), F32)
    for pair in range(width // 128):
        span = slice(128 * pair, 128 * pair + 128)
        pre = conv[:, span]
        x_act = pre * sigmoid(pre)
        step_pair = pair_of(table[...], DT, pair, lane)
        x_step = split(x_act * step_pair)
        grad_out = grad[:, span]
        halves = sides(grad_out, lane)
        pulled = []
        for top, bottom in ((0, half), (half, row_count)):
            pulled_here = jnp.zeros((bottom, 128), F32)
            for side in range(2):
                head = 2 * pair + side
                cum_col = table[top:bottom, CUM + head : CUM + head + 1]
                cum_row = table_t[CUM + head : CUM + head + 1, 0:bottom]
                decay = jnp.exp(cum_col - cum_row + bias[top:bottom, 0:bottom])
                mixing = decay * scores[top:bottom, 0:bottom]
                grad_mix = fine(
                    nt, [part[top:bottom, :] for part in halves[side]], [part[0:bottom, :] for part in x_step]
                )
                grad_scores[top:bottom, 0:bottom] += grad_mix * decay
                turn = grad_mix * mixing
                row_sums[top:bottom, head : head + 1] = jnp.sum(turn, axis=1, keepdims=True)
                col_part = jnp.sum(turn, axis=0, keepdims=True)
                if top == 0:
                    col_sums[head : head + 1, 0:bottom] = col_part
                else:
                    col_sums[head : head + 1, 0:top] += col_part[:, 0:top]
                    col_sums[head : head + 1, top:bottom] = col_part[:, top:bottom]
                pulled_here = pulled_here + tn(mixing.astype(BF16), halves[side][0][top:bottom, :])
            pulled.append(pulled_here)
        grad_step_x = jnp.concatenate([pulled[0] + pulled[1][0:half, :], pulled[1][half:, :]], axis=0)
        grad_x[:, span] = grad_step_x * step_pair + grad_out * skip[:, span]
        step_grad = step_grad + head_sums(grad_step_x * x_act, pair, heads)
        direct_sum = direct_sum + head_sums(grad_out * x_act, pair, heads)
        decayed = grad_out * pair_of(table[...], DECIN, pair, lane)
        state = split(entering[span, :])
        cum_grad = cum_grad + head_sums(decayed * fine(nt, c_act, state), pair, heads)
        grad_c = grad_c + fine(nn, split(decayed), state)
    low_scores = split(grad_scores[...])
    grad_bc[:, 0:NST] = fine(tn, low_scores, c_act)
    grad_bc[:, NST:] = grad_c + fine(nn, low_scores, b_act)
    grad_rows[0:heads, :] = cum_grad + row_sums[...].T[0:heads, :] - col_sums[...]
    grad_rows[heads:, :] = step_grad
    skip_grad[...] = jnp.broadcast_to(jnp.sum(direct_sum, axis=1, keepdims=True), (heads, 128))


def scan_back(ends, idx, conv, table, table_t, grad, entering, params, micro_count, row_count):
    width = grad.shape[1]
    heads = width // P_SIZE
    total = micro_count * row_count
    square = pltpu.VMEM((row_count, row_count), F32)
    return call(
        scan_back_body,
        (micro_count,),
        (ends, idx),
        [conv, table, table_t, grad, entering, params.skip],
        [
            rows(row_count, width + 2 * NST),
            rows(row_count, 128),
            rows(128, row_count),
            rows(row_count, width),
            rows(width, NST),
            whole((1, width)),
        ],
        [
            struct((total, width)),
            struct((total, 2 * NST)),
            struct((micro_count * 2 * heads, row_count)),
            struct((micro_count * heads, 128)),
        ],
        [
            rows(row_count, width),
            rows(row_count, 2 * NST),
            rows(2 * heads, row_count),
            rows(heads, 128),
        ],
        [square, square, square, pltpu.VMEM((row_count, 128), F32), pltpu.VMEM((heads, row_count), F32)],
        flops=100 * total * row_count * heads,
    )


def finish_body(
    idx, conv, table, table_t, grad_x, grad_bc, grad_rows, later, entering, head_cols,
    grad_value, grad_select, grad_step, small, weighted, weighted_low,
):
    row_count, width = grad_x.shape
    heads = width // P_SIZE
    b_pre = conv[:, width : width + NST]
    b_sig = sigmoid(b_pre)
    b_act = split(b_pre * b_sig)
    lane = lax.broadcasted_iota(jnp.int32, (row_count, 128), 1)
    end_grad = jnp.zeros((heads, row_count), F32)
    for pair in range(width // 128):
        span = slice(128 * pair, 128 * pair + 128)
        pre = conv[:, span]
        sig = sigmoid(pre)
        x_act = pre * sig
        end_pair = pair_of(table[...], ENDW, pair, lane)
        reached = fine(nt, b_act, split(later[span, :]))
        end_grad = end_grad + head_sums(x_act * reached, pair, heads)
        weighted[:, span], weighted_low[:, span] = split(x_act * end_pair)
        grad_value[:, span] = (grad_x[:, span] + end_pair * reached) * (
            sig * (1.0 + pre * (1.0 - sig))
        )
    grad_b = grad_bc[:, 0:NST] + fine(nn, (weighted[...], weighted_low[...]), split(later[...]))
    grad_select[:, 0:NST] = grad_b * (b_sig * (1.0 + b_pre * (1.0 - b_sig)))
    c_pre = conv[:, width + NST :]
    c_sig = sigmoid(c_pre)
    grad_select[:, NST:] = grad_bc[:, NST:] * (c_sig * (1.0 + c_pre * (1.0 - c_sig)))

    crossing = (later[...] * entering[...]).reshape(heads, P_SIZE, NST)
    crossing = jnp.sum(jnp.sum(crossing, axis=1), axis=1, keepdims=True)
    end_weighted = end_grad * table_t[ENDW : ENDW + heads, :]
    last = jnp.sum(end_weighted, axis=1, keepdims=True) + crossing * table_t[
        DECIN : DECIN + heads, row_count - 1 : row_count
    ]
    place = lax.broadcasted_iota(jnp.int32, (heads, row_count), 1)
    cum_grad = grad_rows[0:heads, :] - end_weighted + jnp.where(place == row_count - 1, last, 0.0)
    row_id = lax.broadcasted_iota(jnp.int32, (row_count, row_count), 0)
    col_id = lax.broadcasted_iota(jnp.int32, (row_count, row_count), 1)
    grad_decay = nn(cum_grad, (row_id >= col_id).astype(F32), EXACT)
    step_grad = grad_rows[heads:, :] + end_grad * table_t[BASE : BASE + heads, :]
    grad_pre = (step_grad - grad_decay * jnp.exp(head_cols[:, 0:1])) * table_t[SIG : SIG + heads, :]
    small[...] = jnp.zeros_like(small)
    small[:, 0:1] = jnp.sum(grad_pre, axis=1, keepdims=True)
    small[:, 1:2] = jnp.sum(grad_decay * table_t[LOG : LOG + heads, :], axis=1, keepdims=True)
    padded = jnp.concatenate([grad_pre, jnp.zeros((128 - heads, row_count), F32)], axis=0)
    grad_step[...] = padded.T.astype(BF16).astype(F32)


def scan_finish(
    idx, conv, table, table_t, grad_x, grad_bc, grad_rows, later, entering, params, micro_count, row_count
):
    width = grad_x.shape[1]
    heads = width // P_SIZE
    total = micro_count * row_count
    return call(
        finish_body,
        (micro_count,),
        (idx,),
        [conv, table, table_t, grad_x, grad_bc, grad_rows, later, entering, params.head_cols],
        [
            rows(row_count, width + 2 * NST),
            rows(row_count, 128),
            rows(128, row_count),
            rows(row_count, width),
            rows(row_count, 2 * NST),
            rows(2 * heads, row_count),
            rows(width, NST),
            rows(width, NST),
            whole((heads, 128)),
        ],
        [
            struct((total, width)),
            struct((total, 2 * NST)),
            struct((total, 128)),
            struct((micro_count * heads, 128)),
        ],
        [rows(row_count, width), rows(row_count, 2 * NST), rows(row_count, 128), rows(heads, 128)],
        [pltpu.VMEM((row_count, width), BF16), pltpu.VMEM((row_count, width), BF16)],
        flops=60 * total * width,
    )


def taps_back(taps, own_grads, inputs, row_count, span, before, after, tap_grads):
    own = own_grads[0:row_count, span]
    tap_grads[4:5, span] = jnp.sum(own, axis=0, keepdims=True)
    tap_grads[3:4, span] = jnp.sum(own * inputs[8:, span], axis=0, keepdims=True)
    total = own * taps[3:4, span]
    for step in range(1, K):
        tap = K - 1 - step
        tap_grads[tap : tap + 1, span] = jnp.sum(
            own * (inputs[8 - step : 8 - step + row_count, span] * before[step - 1]),
            axis=0,
            keepdims=True,
        )
        total = total + taps[tap : tap + 1, span] * (
            own_grads[step : step + row_count, span] * after[step - 1]
        )
    return total.astype(BF16)


def near_masks(ends, idx, row_count):
    micro = pl.program_id(0)
    at = idx[0] + lax.broadcasted_iota(jnp.int32, (row_count, 1), 0)
    seg = seg_at(at, ends, micro)
    before = [(seg_at(at - step, ends, micro) == seg).astype(F32) for step in range(1, K)]
    after = [(seg_at(at + step, ends, micro) == seg).astype(F32) for step in range(1, K)]
    return (before, after)


def conv_back_body(
    ends, idx, grad_value, halo_value, value, halo_in, taps, gate_part, grad_step, w_value, w_step,
    low_value, tap_grads, c0, c1, c2, c3,
    grads, extended, low, product,
):
    row_count, width = grad_value.shape
    chunk = row_count // 4
    before, after = near_masks(ends, idx, row_count)
    grads[0:row_count, :] = grad_value[...]
    grads[row_count:, :] = halo_value[...]
    extended[0:8, :] = halo_in[...]
    extended[8:, :] = value[...]
    tap_grads[...] = jnp.zeros_like(tap_grads)
    for left in range(0, width, 128):
        span = slice(left, left + 128)
        rounded = taps_back(taps, grads, extended, row_count, span, before, after, tap_grads)
        low[:, span] = rounded
        low_value[:, span] = rounded.astype(F32)
    low_step = grad_step[:, 0 : w_step.shape[1]].astype(BF16)
    for left in range(0, D, 512):
        span = slice(left, left + 512)
        product[:, span] = (
            gate_part[:, span] + nt(low[...], w_value[span, :]) + nt(low_step, w_step[span, :])
        )
    for piece, target in enumerate((c0, c1, c2, c3)):
        place = pl.multiple_of((idx[1] ^ piece) * chunk, chunk)
        target[...] = product[pl.ds(place, chunk), :]


def conv_back(
    ends, idx, grad_value, halo_value, value, halo_in, gate_part, grad_step, params, weights, micro_count, row_count
):
    width = grad_value.shape[1]
    heads = weights.step.shape[1]
    total = micro_count * row_count
    chunk = row_count // 4
    return call(
        conv_back_body,
        (micro_count,),
        (ends, idx),
        [
            grad_value, halo_value, value, halo_in, params.taps, gate_part, grad_step, weights.value,
            weights.step,
        ],
        [
            rows(row_count, width),
            rows(8, width),
            rows(row_count, width),
            rows(8, width),
            whole((8, width)),
            rows(row_count, D),
            rows(row_count, 128),
            whole((D, width)),
            whole((D, heads)),
        ],
        [struct((total, width)), struct((micro_count * 8, width))] + [struct((micro_count * chunk, D))] * 4,
        [rows(row_count, width), rows(8, width)] + [rows(chunk, D)] * 4,
        [
            pltpu.VMEM((row_count + 8, width), F32),
            pltpu.VMEM((row_count + 8, width), F32),
            pltpu.VMEM((row_count, width), BF16),
            pltpu.VMEM((row_count, D), F32),
        ],
        flops=2 * total * width * D,
    )


def select_back_body(
    ends, idx, s0, s1, s2, s3, halo, select, halo_in, taps, grad_step,
    low_select, tap_grads, rest, grads, extended,
):
    row_count, columns = select.shape
    before, after = near_masks(ends, idx, row_count)
    grads[0:row_count, :] = (s0[...] + s1[...]) + (s2[...] + s3[...])
    grads[row_count:, :] = halo[...]
    extended[0:8, :] = halo_in[...]
    extended[8:, :] = select[...]
    tap_grads[...] = jnp.zeros_like(tap_grads)
    for left in range(0, columns, 128):
        span = slice(left, left + 128)
        rounded = taps_back(taps, grads, extended, row_count, span, before, after, tap_grads)
        low_select[:, span] = rounded.astype(F32)
    part = columns // 4
    rest[:, part:] = grad_step[:, 0 : 128 - part]
    for head in range(4):

        @pl.when(idx[1] == head)
        def _():
            rest[:, 0:part] = low_select[:, head * part : (head + 1) * part]


def select_back(ends, idx, selects, halo, select, halo_in, grad_step, params, micro_count, row_count):
    total, columns = select.shape
    right = halo_in.shape[1] // columns - 1
    return call(
        select_back_body,
        (micro_count,),
        (ends, idx),
        [*selects, halo, select, halo_in, params.taps, grad_step],
        [rows(row_count, columns)] * 4
        + [
            rows(8, columns),
            rows(row_count, columns),
            pl.BlockSpec((8, columns), lambda m, *_: (m, right)),
            pl.BlockSpec((8, columns), lambda m, *_: (0, right)),
            rows(row_count, 128),
        ],
        [struct((total, columns)), struct((micro_count * 8, columns)), struct((total, 128))],
        [rows(row_count, columns), rows(8, columns), rows(row_count, 128)],
        [pltpu.VMEM((row_count + 8, columns), F32), pltpu.VMEM((row_count + 8, columns), F32)],
        flops=30 * total * columns,
    )


def weight_body(idx, split, split_other, kept, kept_other, far, own, *, flip):
    def product(a, b):
        return tn(b, a) if flip else tn(a, b)

    low = kept[...].astype(BF16)
    low_other = kept_other[...].astype(BF16)
    result = product(split[...], low) + product(split_other[...].astype(BF16), low_other)

    @pl.when(pl.program_id(0) == 0)
    def _():
        far[...] = result

    @pl.when(pl.program_id(0) == 1)
    def _():
        own[...] = result


def weight_grad(idx, split, split_other, kept, kept_other, flip, marks=()):
    total, width = kept.shape
    block = split.shape[1] // 4
    shape = (width, block) if flip else (block, width)
    return call(
        partial(weight_body, flip=flip),
        (2,),
        (idx,),
        [split, split_other, kept, kept_other],
        [
            pl.BlockSpec((total, block), lambda b, idx: (0, idx[2] ^ (2 - 2 * b))),
            pl.BlockSpec((total, block), lambda b, idx: (0, b)),
            whole((total, width)),
            whole((total, width)),
        ],
        [struct(shape), struct(shape)],
        [whole(shape), whole(shape)],
        flops=8 * total * block * width,
        marks=marks,
    )


def join_body(idx, p0, p1, p2, p3, *refs):
    out = refs[-1]
    chunk = p0.shape[0]
    use_other = idx[3] == 1 if len(refs) > 1 else False

    def from_parts():
        for piece, part in enumerate((p0, p1, p2, p3)):
            out[pl.ds(pl.multiple_of((idx[1] ^ piece) * chunk, chunk), chunk), :] = part[...]

    if len(refs) == 1:
        from_parts()
    else:

        @pl.when(use_other)
        def _():
            out[...] = refs[0][...]

        pl.when(jnp.logical_not(use_other))(from_parts)


def join(idx, parts, other, micro_count, row_count):
    chunk = row_count // 4
    others = [] if other is None else [other]
    return call(
        join_body,
        (micro_count,),
        (idx,),
        [*parts, *others],
        [rows(chunk, D)] * 4 + [rows(row_count, D)] * len(others),
        [struct((micro_count * row_count, D))],
        [rows(row_count, D)],
    )[0]


def after(value, *others):
    return lax.optimization_barrier((value, *others))[0]


def shards(
    block_input,
    out_grad,
    lengths,
    norm_gain,
    gate_weight,
    value_weight,
    select_weight,
    step_weight,
    conv_value,
    conv_value_bias,
    conv_select,
    conv_select_bias,
    step_bias,
    log_rate,
    skip_gain,
    gate_gain,
    output_weight,
):
    micros, row_count, _ = block_input.shape
    total = micros * row_count
    width = gate_weight.shape[2]
    heads = width // P_SIZE
    chunk = row_count // 4
    tok_count = lax.axis_size(TOK)
    section, tok, head = (lax.axis_index(axis) for axis in AXES)
    ends = jnp.cumsum(lengths, axis=1).astype(jnp.int32)

    def scalars(flag, active):
        values = [tok * row_count, head, tok, flag, active]
        return jnp.stack([jnp.asarray(value, jnp.int32) for value in values])

    weights = SimpleNamespace(
        gain=norm_gain,
        gate=gate_weight[0],
        value=value_weight[0],
        select=select_weight[0],
        step=step_weight[0],
        out=output_weight[0],
        gate_gain=gate_gain[0].reshape(1, width),
    )
    taps = jnp.concatenate(
        [
            jnp.concatenate([conv_value[0].reshape(K, width), conv_select[0]], axis=1),
            jnp.concatenate([conv_value_bias[0].reshape(1, width), conv_select_bias], axis=1),
            jnp.zeros((3, width + 2 * NST), F32),
        ],
        axis=0,
    )
    params = SimpleNamespace(
        taps=taps,
        head_rows=jnp.pad(jnp.concatenate([step_bias, log_rate], axis=0), ((0, 6), (0, 128 - heads))),
        head_cols=jnp.pad(log_rate[0][:, None], ((0, 0), (0, 127))),
        skip=jnp.repeat(skip_gain[0], P_SIZE)[None, :],
    )

    def chunk_of(values):
        parts = values.reshape(micros, 4, chunk, values.shape[-1])
        mine = lax.dynamic_index_in_dim(parts, head, 1, keepdims=False)
        return mine.reshape(micros * chunk, values.shape[-1])

    def gather(values, layer):
        return [values] + [to_head(values, layer, step) for step in (1, 2, 3)]

    def reduce_chunks(parts, layer):
        moved = [to_head(parts[step], layer, step) for step in (1, 2, 3)]
        return (parts[0] + moved[0]) + (moved[1] + moved[2])

    def wave(layer, local, table, backward, ahead):
        decay = table.reshape(micros, row_count, 128)[:, row_count - 1, DECIN : DECIN + heads]
        shape = (micros, heads, P_SIZE, NST)
        entering, hops = (None, [])
        for hop in range(tok_count - 1):
            leaving = local
            if entering is not None:
                leaving = (
                    local.reshape(shape) + decay[:, :, None, None] * entering.reshape(shape)
                ).reshape(local.shape)
            source = tok_count - 1 - hop if backward else hop
            target = source - 1 if backward else source + 1

            def move(t, h, source=source, target=target):
                return (target if t == source else -1, h)

            if hop in ahead:
                leaving = after(leaving, *ahead[hop])
            hops.append(send(leaving, layer, move))
            entering = hops[-1] if entering is None else entering + hops[-1]
        return (entering, hops)

    def scan_forward(layer, parts, grads):
        idx = scalars(0, section == layer)
        normed, value, select, step = in_project(idx, parts, weights, micros, row_count)
        edge = jnp.concatenate(
            [
                value.reshape(micros, row_count, width)[:, row_count - 8 :],
                select.reshape(micros, row_count, 2 * NST)[:, row_count - 8 :],
            ],
            axis=-1,
        ).reshape(micros * 8, width + 2 * NST)
        halo = to_tok(edge, layer, 1)
        conv, table, table_t, state = conv_state(
            ends, idx, value, select, step, halo, params, micros, row_count
        )
        gate = gate_project(idx, after(normed, state), weights.gate)
        local = scan_local(ends, idx, conv, table, table_t, params, micros, row_count)
        entering, _ = wave(layer, state, table, False, {1: (gate, local)})
        scan, gated, sums = gate_mix(
            idx, local, conv, table, entering, gate, grads, micros, row_count
        )
        return SimpleNamespace(
            normed=normed, gate=gate, value=value, select=select, halo=halo, conv=conv, table=table,
            table_t=table_t, entering=entering, scan=scan, gated=gated, sums=gather(sums, layer),
        )

    def project_out(layer, saved, marks=()):
        idx = scalars(0, section == layer)
        scaled, *pieces = out_project(idx, saved.gated, saved.sums, weights, micros, row_count, marks)
        return (scaled, reduce_chunks(pieces, layer))

    def exchange(layer, values):
        return send(values, layer, lambda t, h: (t ^ 1, h))

    def split_blocks(values):
        block = values.shape[1] // 4
        return jnp.concatenate(
            [
                lax.dynamic_slice_in_dim(values, (tok ^ 3) * block, block, 1),
                lax.dynamic_slice_in_dim(values, (tok ^ 1) * block, block, 1),
            ],
            axis=1,
        ).astype(F32)

    def pair_product(layer, split, split_other, kept, other, flip=False, hold=(), marks=()):
        idx = scalars(0, section == layer)
        far, own = weight_grad(idx, split, split_other, kept, other, flip, marks)
        return (own, send(after(far, *hold), layer, lambda t, h: (t ^ 2, h)))

    def backward(layer, saved, grads, parts, plan):
        idx = scalars(0, section == layer)
        grad_gate, grad_scan, state, gain_grad, *given = gated_back(
            idx, grads, parts, saved.sums, saved.gate, saved.scan, saved.conv, saved.table, weights,
            micros, row_count,
        )
        state = after(state, *plan.before_wave)
        grad_x, grad_bc, grad_rows, skip_grad = scan_back(
            ends, idx, saved.conv, saved.table, saved.table_t, grad_scan, saved.entering, params,
            micros, row_count,
        )
        gate_part = lax.dot_general(
            after(grad_gate, grad_bc).astype(BF16),
            weights.gate,
            (((1,), (1,)), ((), ())),
            preferred_element_type=F32,
        )
        one, two = plan.in_wave(grad_gate, gate_part, given)
        later, hops = wave(
            layer, state, saved.table, True, {1: (grad_bc, *one), 2: (gate_part, *two)}
        )
        later = after(later, *plan.after_wave(grad_gate, hops))
        grad_value, grad_select, grad_step, small = scan_finish(
            idx, saved.conv, saved.table, saved.table_t, grad_x, grad_bc, grad_rows, later,
            saved.entering, params, micros, row_count,
        )
        first_value = grad_value.reshape(micros, row_count, width)[:, :8].reshape(micros * 8, width)
        halo_value = to_tok(first_value, layer, -1)
        selects = gather(grad_select, layer)
        first_select = grad_select.reshape(micros, row_count, 2 * NST)[:, :8].reshape(micros * 8, 2 * NST)
        halos = [
            send(first_select, layer, lambda t, h, step=step: (t - 1, h ^ step)) for step in range(4)
        ]
        waits = (*halos, *plan.before_conv(grad_step, (halo_value, *halos)))
        low_value, value_taps, *pieces = conv_back(
            ends, idx, after(grad_value, *waits), halo_value, saved.value, saved.halo, gate_part, grad_step,
            params, weights, micros, row_count,
        )
        grad_sum = reduce_chunks(pieces, layer)
        selects = [selects[0]] + [after(part, grad_sum) for part in selects[1:]]
        halo_select = sum(halos)
        grad_normed = after(grad_sum, *plan.beside_sum(pieces[0], low_value))
        low_select, select_taps, rest = select_back(
            ends, idx, selects, halo_select, saved.select, saved.halo, grad_step, params, micros, row_count
        )
        grad_normed = grad_normed + lax.dot_general(
            chunk_of(low_select).astype(BF16),
            weights.select,
            (((1,), (1,)), ((), ())),
            preferred_element_type=F32,
        )
        hidden = saved.chunk_in
        inv = lax.rsqrt(jnp.mean(hidden * hidden, axis=-1, keepdims=True) + EPSILON)
        norm_grad = jnp.sum(grad_normed * hidden * inv, axis=0)
        weighted = grad_normed * weights.gain
        grad_hidden = (
            saved.grad_chunk
            + inv * weighted
            - hidden * (inv * inv * inv) * jnp.mean(weighted * hidden, axis=-1, keepdims=True)
        )
        sums = (
            norm_grad,
            jnp.concatenate(
                [
                    value_taps.reshape(micros, 8, -1)[:, : K + 1].sum(0).reshape(-1),
                    select_taps.reshape(micros, 8, -1)[:, : K + 1].sum(0).reshape(-1),
                    gain_grad.reshape(micros, 8, -1)[:, 0].sum(0),
                    small.reshape(micros, heads, 128).sum(0)[:, :2].T.reshape(-1),
                    skip_grad.reshape(micros, heads, 128).sum(0)[:, 0],
                ]
            ),
        )
        return (grad_hidden, SimpleNamespace(gate=grad_gate, value=low_value, rest=rest), sums)

    first = section == 0
    pairwise = tok_count == 4
    grad_rows_1 = out_grad.reshape(total, D)
    scaled_grads_1 = back_project(scalars(0, section == 1), grad_rows_1, weights.out, micros, row_count)

    input_rows = block_input.reshape(total, D)
    saved_0 = scan_forward(0, [input_rows], [])
    saved_0.chunk_in = chunk_of(input_rows).astype(F32)
    saved_0.scaled, saved_0.branch = project_out(0, saved_0)
    out_0 = moved = saved_0.chunk_in + saved_0.branch
    if pairwise:
        grad_other_1 = exchange(1, split_blocks(grad_rows_1))
        moved = after(out_0, grad_other_1, scaled_grads_1)

    chunk_1 = lax.ppermute(moved, SECTION, [(0, 1)])
    parts_1 = gather(chunk_1, 1)
    if pairwise:
        other_0 = exchange(0, after(split_blocks(saved_0.normed), out_0))
        scaled_0 = exchange(0, after(saved_0.scaled, out_0))
        parts_1[0] = after(parts_1[0], other_0, scaled_0)
    saved_1 = scan_forward(1, parts_1, [scaled_grads_1, weights.gate_gain])
    saved_1.chunk_in = chunk_1
    saved_1.grad_chunk = chunk_of(grad_rows_1).astype(F32)

    work = SimpleNamespace()
    before_wave_1 = ()
    if pairwise:
        other_1 = exchange(1, after(split_blocks(saved_1.normed), saved_1.entering))
        before_wave_1 = (other_1,)

    def in_wave_1(grad_gate, gate_part, given):
        saved_1.scaled = given[0]
        work.kept_gate = grad_gate
        return ((), ())

    def after_wave_1(grad_gate, hops):
        if pairwise:
            work.gate_other = exchange(1, after(grad_gate, hops[0]))
        return ()

    def before_conv_1(done, halo):
        if not pairwise:
            return ()
        work.gate_1 = pair_product(
            1, saved_1.normed, other_1, after(work.kept_gate, done), work.gate_other, hold=halo
        )
        return (work.gate_1[0],)

    def beside_sum_1(piece, low_value):
        if pairwise:
            work.value_other = exchange(1, low_value)
            return (work.gate_1[1], work.value_other)
        return ()

    grad_mid, kept_1, sums_1 = backward(
        1, saved_1, scaled_grads_1, None,
        SimpleNamespace(
            before_wave=before_wave_1, in_wave=in_wave_1, after_wave=after_wave_1, before_conv=before_conv_1,
            beside_sum=beside_sum_1,
        ),
    )

    saved_0.grad_chunk = lax.ppermute(grad_mid, SECTION, [(1, 0)])
    low_chunk = lax.reduce_precision(saved_0.grad_chunk, 8, 7)
    inner = jnp.sum(low_chunk * saved_0.branch, axis=-1, keepdims=True) / (H * P_SIZE)
    payload = jnp.concatenate(
        [saved_0.grad_chunk, jnp.broadcast_to(inner, (micros * chunk, PAD))], axis=1
    )
    parts_0 = gather(payload, 0)
    before_wave_0 = ()
    if pairwise:
        work.value_1 = pair_product(
            1, saved_1.normed, other_1, kept_1.value, after(work.value_other, grad_mid)
        )
        scaled_other = exchange(1, after(saved_1.scaled, grad_mid))
        work.scaled_1 = pair_product(
            1, grad_rows_1, grad_other_1, after(saved_1.scaled, work.value_1[0]), scaled_other, True
        )
        parts_0[0] = after(parts_0[0], work.value_1[0])

    def tell(values):
        return lax.ppermute(values[:8, :128], SECTION, [(0, 1)])

    def in_wave_0(grad_gate, gate_part, given):
        work.low_grad_0, work.full_0 = given
        work.kept_gate_0 = grad_gate
        marks = (work.value_1[1][:8, :128],) if pairwise else ()
        _, branch = project_out(1, saved_1, marks)
        work.out_1 = chunk_1 + branch
        work.shown_1 = gather(work.out_1, 1)
        return ((), ())

    def after_wave_0(grad_gate, hops):
        if not pairwise:
            return (work.out_1,)
        work.gate_other_0 = exchange(0, after(grad_gate, hops[0]))
        work.grad_other_0 = exchange(0, after(split_blocks(work.low_grad_0), hops[-1]))
        return (work.out_1,)

    def before_conv_0(done, halo):
        if not pairwise:
            return ()
        work.gate_0 = pair_product(
            0, saved_0.normed, other_0, after(work.kept_gate_0, done), work.gate_other_0, hold=halo
        )
        return (work.gate_0[0], work.scaled_1[1], *work.shown_1)

    def beside_sum_0(piece, low_value):
        if not pairwise:
            return ()
        work.value_other_0 = exchange(0, low_value)
        work.scaled_0 = pair_product(
            0, work.low_grad_0, work.grad_other_0, after(saved_0.scaled, piece), scaled_0, True
        )
        return (work.scaled_0[0],)

    grad_in, kept_0, sums_0 = backward(
        0, saved_0, None, parts_0,
        SimpleNamespace(
            before_wave=before_wave_0, in_wave=in_wave_0, after_wave=after_wave_0, before_conv=before_conv_0,
            beside_sum=beside_sum_0,
        ),
    )
    shown_0 = gather(grad_in, 0)

    def chosen(left, right):
        return jnp.where(first, left, right)

    rest_sum = chosen(
        tn(saved_0.normed, kept_0.rest.astype(BF16)), tn(saved_1.normed, kept_1.rest.astype(BF16))
    )
    norm_sum, head_sum = (chosen(left, right) for left, right in zip(sums_0, sums_1, strict=True))
    packed = jnp.concatenate([norm_sum, head_sum])
    size = -(-packed.size // 1024) * 1024
    packed = jnp.pad(packed, (0, size - packed.size)).reshape(-1, 128)
    block = D // tok_count

    def block_of(which):
        return lax.dynamic_slice_in_dim(rest_sum, which * block, block, 0)

    if pairwise:
        total_sum = jnp.concatenate([block_of(tok), packed], axis=0)
        for step in (1, 2, 3):
            total_sum = total_sum + lax.ppermute(
                jnp.concatenate([block_of(tok ^ step), packed], axis=0),
                TOK,
                [(source, source ^ step) for source in range(4)],
            )
        rest_sum, packed = (total_sum[:block], total_sum[block:])
    else:
        rest_sum = lax.psum_scatter(rest_sum, TOK, scatter_dimension=0, tiled=True)
        packed = lax.psum(packed, TOK)
    quarter = 2 * NST // 4
    packed = packed.reshape(-1)
    norm_sum, head_sum = (lax.dynamic_slice_in_dim(packed[:D], tok * block, block, 0), packed[D:])
    lanes = jnp.concatenate(
        [rest_sum[:, :quarter], jnp.broadcast_to(norm_sum[:, None], (block, 128 - quarter))], axis=1
    )
    norm_sum = norm_sum[:, None]
    select_sum = jnp.zeros((block, 2 * NST), F32)
    for step in range(4):
        moved = lanes
        if step > 0:
            moved = lax.ppermute(lanes, HEAD, [(source, source ^ step) for source in range(4)])
            norm_sum = norm_sum + moved[:, quarter : quarter + 1]
        select_sum = lax.dynamic_update_slice_in_dim(
            select_sum, moved[:, :quarter], (head ^ step) * quarter, 1
        )
    norm_sum = norm_sum[:, 0]

    if pairwise:
        work.value_0 = pair_product(
            0, saved_0.normed, other_0, after(kept_0.value, grad_in, work.scaled_0[1]), work.value_other_0
        )
        parts_1[0] = after(parts_1[0], work.value_0[0])
        work.full_0 = after(work.full_0, work.value_0[0])
    full_1 = join(scalars(0, section == 1), parts_1, None, micros, row_count)
    layer_out = join(
        scalars(first, 1), work.shown_1, lax.ppermute(full_1, SECTION, [(1, 0)]), micros, row_count
    )
    full_0 = lax.ppermute(work.full_0, SECTION, [(0, 1)])
    input_grad = join(scalars(section == 1, 1), shown_0, full_0, micros, row_count)
    if pairwise:
        scaled_sum, gate_sum, value_sum = (
            chosen(left[0] + after(left[1], *waits), right[0] + right[1])
            for left, right, waits in (
                (work.scaled_0, work.scaled_1, ()),
                (work.gate_0, work.gate_1, ()),
                (work.value_0, work.value_1, (select_sum, layer_out, input_grad)),
            )
        )
    else:
        normed = chosen(saved_0.normed, saved_1.normed)

        def scattered(left, right, axis):
            return lax.psum_scatter(
                tn(left.astype(BF16), right.astype(BF16)), TOK, scatter_dimension=axis, tiled=True
            )

        scaled_sum = scattered(
            chosen(saved_0.scaled, saved_1.scaled), chosen(work.low_grad_0, grad_rows_1), 1
        )
        gate_sum, value_sum = (
            scattered(normed, chosen(left, right), 0)
            for left, right in ((kept_0.gate, kept_1.gate), (kept_0.value, kept_1.value))
        )
    pieces, place = ([], 0)
    for shape in ((K + 1, width), (K + 1, 2 * NST), (heads, P_SIZE), (heads,), (heads,), (heads,)):
        size = 1
        for extent in shape:
            size *= extent
        pieces.append(head_sum[place : place + size].reshape(shape))
        place += size
    value_taps, select_taps, gain_sum, bias_sum, rate_sum, skip_sum = pieces

    def mine(values, axis):
        size = values.shape[axis] // tok_count
        return lax.dynamic_slice_in_dim(values, tok * size, size, axis)

    outs = (
        layer_out.reshape(micros, row_count, D),
        input_grad.reshape(micros, row_count, D),
        norm_sum,
        gate_sum,
        value_sum,
        select_sum,
        rest_sum[:, quarter : quarter + heads],
        mine(value_taps[:K].reshape(K, heads, P_SIZE), 2),
        mine(value_taps[K].reshape(heads, P_SIZE), 1),
        mine(select_taps[:K], 1),
        mine(select_taps[K], 0),
        bias_sum,
        rate_sum,
        skip_sum,
        mine(gain_sum, 1),
        scaled_sum,
    )
    return tuple(value[None] for value in outs)


def solution(mesh):
    return jax.shard_map(
        shards,
        mesh=mesh,
        in_specs=(
            P(None, TOK, None),
            P(None, TOK, None),
            P(),
            P(SECTION, None),
            P(SECTION, None, HEAD),
            P(SECTION, None, HEAD),
            P(SECTION, None, None),
            P(SECTION, None, HEAD),
            P(SECTION, None, HEAD, None),
            P(SECTION, HEAD, None),
            P(SECTION, None, None),
            P(SECTION, None),
            P(SECTION, HEAD),
            P(SECTION, HEAD),
            P(SECTION, HEAD),
            P(SECTION, HEAD, None),
            P(SECTION, HEAD, None),
        ),
        out_specs=(
            P(SECTION, None, TOK, None),
            P(SECTION, None, TOK, None),
            P(SECTION, TOK),
            P(SECTION, TOK, HEAD),
            P(SECTION, TOK, HEAD),
            P(SECTION, TOK, None),
            P(SECTION, TOK, HEAD),
            P(SECTION, None, HEAD, TOK),
            P(SECTION, HEAD, TOK),
            P(SECTION, None, TOK),
            P(SECTION, TOK),
            P(SECTION, HEAD),
            P(SECTION, HEAD),
            P(SECTION, HEAD),
            P(SECTION, HEAD, TOK),
            P(SECTION, HEAD, TOK),
        ),
        check_vma=False,
    )
```
